128 devices in a mesh: gx: 16 (over y, z), gy: 8 (over x, core).
Axes of the slice: x: 4, y: 4, z: 4, core: 2. Of those that a mesh axis runs over, the one named last changes fastest.
Arguments:
- phase_one: float32 [4, 2, 2048, 1024], P(None, None, 'gx', 'gy'), may hold values from -3.140625 to 3.140625
- phase_two: float32 [4, 2, 2048, 1024], P(None, None, 'gx', 'gy'), may hold values from -3.140625 to 3.140625
- hop_one: float32 [3, 2048, 1024], P(None, 'gx', 'gy'), may hold values from 0.08 to 0.16
- hop_two: float32 [3, 2048, 1024], P(None, 'gx', 'gy'), may hold values from 0.08 to 0.16
- onsite_one: float32 [2, 2048, 1024], P(None, 'gx', 'gy'), may hold values from -0.25 to 0.25
- onsite_two: float32 [2, 2048, 1024], P(None, 'gx', 'gy'), may hold values from -0.25 to 0.25
- coupling: float32 [16, 8, 8, 2, 16, 2, 16], P('gx', 'gy'), may hold values from -0.3 to 0.3
- owner: int32 [16, 8, 8], P('gx', 'gy'), may hold values from 0 to 127, as said below
- target_row: int32 [16, 8, 8], P('gx', 'gy'), may hold values from 0 to 112
- live_strips: int32 [16, 8], P('gx', 'gy'), may hold values from 1 to 8, as said below
Outputs:
- first_two: float32 [4, 2, 2, 2048, 1024], P(None, None, None, 'gx', 'gy')
- second_two: float32 [4, 2, 2, 2048, 1024], P(None, None, None, 'gx', 'gy')
- first_three: float32 [4, 2, 2, 2048, 1024], P(None, None, None, 'gx', 'gy')
- second_three: float32 [4, 2, 2, 2048, 1024], P(None, None, None, 'gx', 'gy')
The draws below stay inside these ranges and needn't reach their ends.
Inputs may be any that keep to these rules, and one draw needn't show every extreme that they name: owner[i, j, k] = gi * 8 + gj, where gi and gj differ from i and j by at most one. `live_strips`: some block holds all 8 strips.
All inputs are finite; a program needn't handle non-finite values.
Results may differ from the reference program's by a relative error of at most 0.003.
Values may be sent and summed in bfloat16 or wider, within the bound.
No kernel may reach another device: no remote copies, remote signals or barrier semaphores. Data moves between devices by JAX's collectives and lax.ppermute only.
A program may use at most 128 MiB of HBM per device.

```python
import jax
import jax.numpy as jnp
from jax import lax

STATES = 4
TILE = 128
SR = 16
NSTRIP = 8
NX = 2048
NY = 1024
N_GX = 16
N_GY = 8


def intersection_geometry(key):
    key_relax, key_wall = jax.random.split(key)
    relax = jax.random.randint(key_relax, (N_GX, N_GY, 1), -SR, SR + 1)
    wall = jax.random.randint(key_wall, (N_GX, 1, 1), -1, 2)
    row_block = jnp.arange(N_GX, dtype=jnp.int32)[:, None, None]
    col_block = jnp.arange(N_GY, dtype=jnp.int32)[None, :, None]
    strip_k = jnp.arange(NSTRIP, dtype=jnp.int32)[None, None, :]
    offset = (2 * col_block + 1 - N_GY) * 3 * TILE // (4 * N_GY) + relax
    global_row = jnp.clip(row_block * TILE + strip_k * SR + offset, 0, NX - SR)
    owner_row = global_row // TILE
    inside = jnp.minimum(global_row % TILE, TILE - SR)
    drift = jnp.clip((2 * row_block + 1 - N_GX) * 3 // (2 * N_GX) + wall, -1, 1)
    owner_col = jnp.clip(col_block + drift, 0, N_GY - 1)
    owners = owner_row * N_GY + owner_col + 0 * strip_k
    return (owners.astype(jnp.int32), inside.astype(jnp.int32))


def draw_owner(key, part):
    owners, inside = intersection_geometry(key)
    return owners


def draw_target_row(key, part):
    owners, inside = intersection_geometry(key)
    return inside


def draw_live_strips(key, part):
    key = jax.random.fold_in(key, 11)
    row_block = jnp.arange(N_GX, dtype=jnp.int32)[:, None]
    col_block = jnp.arange(N_GY, dtype=jnp.int32)[None, :]
    border = (row_block == 0) | (row_block == N_GX - 1) | (col_block == 0) | (col_block == N_GY - 1)
    counts = jax.random.randint(key, (N_GX, N_GY), 1, NSTRIP + 1)
    return jnp.where(border, counts, NSTRIP).astype(jnp.int32)


def levels(stream_key, shape, shards, low, largest):
    gain, own = 1.0, jax.random.fold_in(stream_key, 6)
    for position, shards_of in shards:
        heights = jnp.exp(jax.random.uniform(jax.random.fold_in(own, position), (shards_of,), jnp.float32, low / len(shards), largest / len(shards)))
        gain = gain * jnp.repeat(heights, shape[position] // shards_of).reshape([-1 if axis == position else 1 for axis in range(len(shape))])
    return gain


def gaussian(key, extent, scale, limit, cuts=(), held_as=jnp.bfloat16):
    result = jax.random.normal(key, extent, jnp.float32) * scale
    if len(cuts) > 0:
        result = levels(key, extent, cuts, -0.22, 0.18) * result
    return jnp.clip(result, min=-limit, max=limit).astype(held_as)


def setup_inputs(seed: int = 0) -> dict:
    streams_of = jax.random.split(jax.random.key(seed), 11)
    phase_one = jnp.clip(jax.random.uniform(streams_of[0], (STATES, 2, NX, NY), jnp.float32, -3.140625, 3.140625), -3.140625, 3.140625)
    phase_two = jnp.clip(jax.random.uniform(streams_of[1], (STATES, 2, NX, NY), jnp.float32, -3.140625, 3.140625), -3.140625, 3.140625)
    hop_one = jnp.clip(0.08 + 0.08 * jax.random.uniform(streams_of[2], (3, NX, NY), jnp.float32) ** levels(streams_of[2], (3, NX, NY), ((1, 16), (2, 8)), -0.2, 0.2), 0.08, 0.16)
    hop_two = jnp.clip(0.08 + 0.08 * jax.random.uniform(streams_of[3], (3, NX, NY), jnp.float32) ** levels(streams_of[3], (3, NX, NY), ((1, 16), (2, 8)), -0.2, 0.2), 0.08, 0.16)
    onsite_one = jnp.clip(jax.random.uniform(streams_of[4], (2, NX, NY), jnp.float32, -0.25, 0.25) * levels(streams_of[4], (2, NX, NY), ((1, 16), (2, 8)), -0.4, 0.0), -0.25, 0.25)
    onsite_two = jnp.clip(jax.random.uniform(streams_of[5], (2, NX, NY), jnp.float32, -0.25, 0.25) * levels(streams_of[5], (2, NX, NY), ((1, 16), (2, 8)), -0.4, 0.0), -0.25, 0.25)
    coupling = gaussian(streams_of[6], (N_GX, N_GY, NSTRIP, 2, SR, 2, SR), 0.05, 0.3, ((0, 16), (1, 8)), jnp.float32)
    owner = draw_owner(jax.random.fold_in(streams_of[10], 71), 0)
    target_row = draw_target_row(jax.random.fold_in(streams_of[10], 71), 0)
    live_strips = draw_live_strips(jax.random.fold_in(streams_of[10], 71), 0)
    return dict(phase_one=phase_one, phase_two=phase_two, hop_one=hop_one, hop_two=hop_two, onsite_one=onsite_one, onsite_two=onsite_two, coupling=coupling, owner=owner, target_row=target_row, live_strips=live_strips)


HIGHEST_PRECISION = lax.Precision.HIGHEST


def intralayer(field, padded, hopping, hop_padded, onsite):
    upper = onsite[0] * field[:, :, 0] + hopping[0] * field[:, :, 1] + hopping[1] * padded[:, :, 1, :-2, 1:-1] + hopping[2] * padded[:, :, 1, 1:-1, :-2]
    lower = onsite[1] * field[:, :, 1] + hopping[0] * field[:, :, 0] + hop_padded[1, 2:, 1:-1] * padded[:, :, 0, 2:, 1:-1] + hop_padded[2, 1:-1, 2:] * padded[:, :, 0, 1:-1, 2:]
    return jnp.stack([upper, lower], axis=2)


def interlayer(first, second, coupling, owner, target_row, live_strips):
    count = N_GX * N_GY * NSTRIP
    sizes = (STATES, 2, 2, SR, TILE)
    zero = jnp.zeros((), jnp.int32)

    def visit(index, carry):
        out_first, out_second = carry
        index = jnp.asarray(index).astype(jnp.int32)
        tile_x = index // (N_GY * NSTRIP)
        tile_y = (index // NSTRIP) % N_GY
        strip_k = index % NSTRIP
        active = (strip_k < live_strips[tile_x, tile_y]).astype(jnp.float32)
        weights = coupling[tile_x, tile_y, strip_k] * active
        target = owner[tile_x, tile_y, strip_k].astype(jnp.int32)
        row_one = ((target // N_GY) * TILE + target_row[tile_x, tile_y, strip_k]).astype(jnp.int32)
        col_one = ((target % N_GY) * TILE).astype(jnp.int32)
        row_two = (tile_x * TILE + strip_k * SR).astype(jnp.int32)
        col_two = (tile_y * TILE).astype(jnp.int32)
        start_one = (zero, zero, zero, row_one, col_one)
        start_two = (zero, zero, zero, row_two, col_two)
        source_one = lax.dynamic_slice(first, start_one, sizes)
        source_two = lax.dynamic_slice(second, start_two, sizes)
        add_one = jnp.einsum('apbq,xybqc->xyapc', weights, source_two, precision=HIGHEST_PRECISION)
        add_two = jnp.einsum('apbq,xyapc->xybqc', weights, source_one, precision=HIGHEST_PRECISION)
        out_first = lax.dynamic_update_slice(out_first, lax.dynamic_slice(out_first, start_one, sizes) + add_one, start_one)
        out_second = lax.dynamic_update_slice(out_second, lax.dynamic_slice(out_second, start_two, sizes) + add_two, start_two)
        return out_first, out_second

    empty = jnp.zeros(first.shape, jnp.float32)
    return lax.fori_loop(0, count, visit, (empty, empty))


def hamiltonian(first, second, hop_one, hop_two, onsite_one, onsite_two, coupling, owner, target_row, live_strips):
    first_b, second_b = lax.optimization_barrier((first.astype(jnp.bfloat16), second.astype(jnp.bfloat16)))
    field_one = first_b.astype(jnp.float32)
    field_two = second_b.astype(jnp.float32)
    widths = ((0, 0), (0, 0), (0, 0), (1, 1), (1, 1))
    bond_widths = ((0, 0), (1, 1), (1, 1))
    own_one = intralayer(field_one, jnp.pad(field_one, widths), hop_one, jnp.pad(hop_one, bond_widths), onsite_one)
    own_two = intralayer(field_two, jnp.pad(field_two, widths), hop_two, jnp.pad(hop_two, bond_widths), onsite_two)
    cross_one, cross_two = interlayer(field_one, field_two, coupling, owner, target_row, live_strips)
    return own_one + cross_one, own_two + cross_two


def reference(phase_one, phase_two, hop_one, hop_two, onsite_one, onsite_two, coupling, owner, target_row, live_strips):
    zero_one = jnp.stack([jnp.cos(phase_one), jnp.sin(phase_one)], axis=1)
    zero_two = jnp.stack([jnp.cos(phase_two), jnp.sin(phase_two)], axis=1)
    extra = (hop_one, hop_two, onsite_one, onsite_two, coupling, owner, target_row, live_strips)
    one_a, one_b = hamiltonian(zero_one, zero_two, *extra)
    image_a, image_b = hamiltonian(one_a, one_b, *extra)
    two_a = 2.0 * image_a - zero_one
    two_b = 2.0 * image_b - zero_two
    image_a, image_b = hamiltonian(two_a, two_b, *extra)
    three_a = 2.0 * image_a - one_a
    three_b = 2.0 * image_b - one_b
    return two_a, two_b, three_a, three_b
```

```python
import math

import jax
import jax.numpy as jnp
from jax import lax
from jax.experimental import pallas as pl
from jax.experimental.pallas import tpu as pltpu
from jax.sharding import PartitionSpec as P

RING = 4
T = 128
KS = 8
SR = 16
HALO = RING + 2
HOMES = HALO * 3
F32 = jnp.float32
BF16 = jnp.bfloat16
I16 = jnp.int16
PHASE_UNIT = math.pi / 32768.0
HOP_MID, HOP_UNIT = 0.12, 0.04 / 32767.0
SITE_UNIT = 0.25 / 32767.0
COUPLING_UNIT = 0.3 / 32767.0
VMEM_LIMIT = 56 * 1024 * 1024


def coded(values, unit):
    return jnp.clip(jnp.round(values * (1.0 / unit)), -32768.0, 32767.0).astype(I16)


def moved(array, axis, by):
    size = lax.axis_size(axis)
    return lax.ppermute(array, axis, [(i, i + by) for i in range(size) if 0 <= i + by < size])


def ring_moved(array, by):
    size = lax.axis_size("gx")
    pairs = [(i, i // RING * RING + (i + by) % RING) for i in range(size)]
    return lax.ppermute(array, "gx", pairs)


def ring_scattered(array, z):
    parts = [lax.dynamic_index_in_dim(array, z, 0, False)]
    for d in range(1, RING):
        sent = lax.dynamic_index_in_dim(array, (z + d) % RING, 0, False)
        parts.append(ring_moved(sent, d))
    return parts


def ring_gathered(array):
    return [array] + [ring_moved(array, d) for d in range(1, RING)]


def ordered(parts, z):
    back = jnp.stack(parts[::-1] + parts[::-1])
    return lax.dynamic_slice_in_dim(back, RING - 1 - z, RING, 0)


def lane_iota(shape, dim):
    return lax.broadcasted_iota(jnp.int32, shape, dim)


def build_kernel(small, bd1, bd2):
    rows, cols = lane_iota((32, 256), 0), lane_iota((32, 256), 1)
    place = ((rows // 16 == cols // 128) & (rows % 16 == cols % 16)).astype(BF16)
    i, j = lane_iota((256, 256), 0), lane_iota((256, 256), 1)
    mask1 = (i // 32) == ((j // 16) % 8)
    mask2 = ((i // 16) % 8) == (j // 32)
    first = (((0,), (0,)), ((), ()))

    def spread(left, right, mask):
        full = lax.dot_general(left, right, first, preferred_element_type=F32)
        return jnp.where(mask, full, 0.0).astype(BF16)

    for home in range(HOMES):
        c = small[home, 0:32, :].astype(jnp.int32).astype(F32) * COUPLING_UNIT
        high = c.astype(BF16)
        low = (c - high.astype(F32)).astype(BF16)
        bd1[home, 0:256, :] = spread(high, place, mask1)
        bd1[home, 256:512, :] = spread(low, place, mask1)
        rb, cb = divmod(home, 3)
        if cb == 1 and 1 <= rb <= RING:
            bd2[rb - 1, 0:256, :] = spread(place, high, mask2)
            bd2[rb - 1, 256:512, :] = spread(place, low, mask2)


def operators_kernel(z_ref, part0, part1, part2, part3, ops):
    z = z_ref[0, 0]
    lane = lane_iota((T, T), 1)
    for d, part in enumerate((part0, part1, part2, part3)):
        at = pl.ds(pl.multiple_of((z + RING - d) % RING * T, T), T)
        edges = part[10 * T : 10 * T + 16, :].astype(jnp.int32).astype(F32) * HOP_UNIT + HOP_MID
        for layer in range(2):
            base = layer * 5

            def raw(n):
                return part[(base + n) * T : (base + n + 1) * T, :].astype(jnp.int32).astype(F32)

            h = [raw(n) * HOP_UNIT + HOP_MID for n in range(3)]
            for n in range(3):
                ops[layer, n, at, :] = h[n]
            for n in range(2):
                ops[layer, 3 + n, at, :] = raw(3 + n) * SITE_UNIT
            ops[layer, 5, at, :] = jnp.concatenate([h[1][1:, :], edges[layer : layer + 1, :]], 0)
            column = jnp.broadcast_to(edges[2 + layer : 3 + layer, :], (T, T)).T
            ops[layer, 6, at, :] = jnp.where(lane == T - 1, column, pltpu.roll(h[2], T - 1, 1))


def cos_sin(code):
    q = code.astype(jnp.int32)
    quarter = (q + 8192) >> 14
    r = (q - (quarter << 14)).astype(F32) * PHASE_UNIT
    r2 = r * r
    s = r * (1.0 + r2 * (-1.6666654611e-1 + r2 * (8.3321608736e-3 + r2 * -1.9515295891e-4)))
    c = 1.0 + r2 * (-0.5 + r2 * (4.166664568298827e-2 + r2 * (-1.388731625493765e-3 + r2 * 2.443315711809948e-5)))
    odd = (quarter & 1) == 1
    cos_v = jnp.where(odd, s, c)
    sin_v = jnp.where(odd, c, s)
    cos_v = jnp.where(((quarter + 1) & 2) == 2, -cos_v, cos_v)
    sin_v = jnp.where((quarter & 2) == 2, -sin_v, sin_v)
    return cos_v, sin_v


def step_kernel(first, last, *refs):
    refs = list(refs)
    idx, own, left, right, top, bottom, lcorner, rcorner, bd1, bd2, ops = refs[:11]
    refs = refs[11:]
    prev = None if first else refs.pop(0)
    if first:
        zero_out, wide_out, narrow_out = refs[:3]
        refs = refs[3:]
    else:
        narrow_out = refs.pop(0)
    fu, fv, gathered, terms, acc1, acc2 = refs[:6]
    xv = refs[6] if first else None

    def block(layer, rb, cb):
        if 1 <= rb <= RING:
            return (left, own, right)[cb].at[rb - 1, layer]
        if cb == 1:
            return (top if rb == 0 else bottom).at[layer]
        return (lcorner if cb == 0 else rcorner).at[0 if rb == 0 else 1, layer]

    for cb in range(3):
        for rb in range(HALO):
            rows = slice(rb * T, (rb + 1) * T)
            for layer in range(2):
                ref = block(layer, rb, cb)
                for a in range(2):
                    if first:
                        pair = cos_sin(ref[a])
                        if cb == 1 and 1 <= rb <= RING:
                            for p in range(2):
                                zero_out[layer, a, p, (rb - 1) * T : rb * T, :] = pair[p]
                        keep = None
                        if cb != 1:
                            keep = idx[0, 240 + (2 if cb == 0 else 3)]
                        elif rb in (0, HALO - 1):
                            keep = idx[0, 240 + (0 if rb == 0 else 1)]
                        if keep is not None:
                            keep = keep.astype(F32)
                            pair = tuple(v * keep for v in pair)
                        pair = tuple(v.astype(BF16) for v in pair)
                        if layer == 1:
                            for p in range(2):
                                xv[rb * 3 + cb, a * T : (a + 1) * T, p * T : (p + 1) * T] = pair[p]
                    else:
                        if layer == 1 and cb != 1:
                            continue
                        pair = tuple(ref[a * T : (a + 1) * T, p * T : (p + 1) * T] for p in range(2))
                    for p in range(2):
                        if layer == 0:
                            fu[cb, a, p, rows, :] = pair[p].astype(F32)
                        elif cb == 1:
                            fv[a, p, rows, :] = pair[p].astype(F32)

    for r in range(RING):
        for k in range(KS):
            row = idx[0, 164 + r * KS + k]
            col = idx[0, 200 + r * KS + k]
            for a in range(2):
                for p in range(2):
                    piece = fu[col, a, p, pl.ds(row, SR), :].astype(BF16)
                    gathered[k * 32 + a * SR : k * 32 + (a + 1) * SR, p * T : (p + 1) * T] = piece
        both = jnp.dot(bd2[r], gathered[...], preferred_element_type=F32)
        summed = both[:256] + both[256:]
        for b in range(2):
            for p in range(2):
                acc2[b, p, r * T : (r + 1) * T, :] = summed[b * T : (b + 1) * T, p * T : (p + 1) * T]

    acc1[...] = jnp.zeros_like(acc1)
    for home in range(HOMES):
        rb, cb = divmod(home, 3)

        @pl.when(idx[0, 144 + home] > 0)
        def _():
            source = xv[home] if first else block(1, rb, cb)[...]
            both = jnp.dot(bd1[home], source, preferred_element_type=F32)
            terms[...] = both[:256] + both[256:]
            for k in range(KS):
                row = idx[0, home * KS + k]

                @pl.when(row >= 0)
                def _():
                    for a in range(2):
                        for p in range(2):
                            at = (a, p, pl.ds(row, SR), slice(None))
                            acc1[at] = acc1[at] + terms[
                                k * 32 + a * SR : k * 32 + (a + 1) * SR, p * T : (p + 1) * T
                            ]

    lane = lane_iota((T, T), 1)
    for layer in range(2):
        acc = (acc1, acc2)[layer]

        def field(a, p, low):
            if layer == 0:
                return fu[1, a, p, low : low + T, :]
            return fv[a, p, low : low + T, :]

        def beside(a, p, r, cb):
            if layer == 0:
                return fu[cb, a, p, (r + 1) * T : (r + 2) * T, :]
            where = (slice(a * T, (a + 1) * T), slice(p * T, (p + 1) * T))
            if first:
                return xv[(r + 1) * 3 + cb, where[0], where[1]].astype(F32)
            return (left, own, right)[cb][r, 1, where[0], where[1]].astype(F32)

        for r in range(RING):
            rows = slice(r * T, (r + 1) * T)
            h0, h1, h2, e0, e1, h1s, h2s = [ops[layer, n, rows, :] for n in range(7)]
            for p in range(2):
                base = (r + 1) * T
                w0, w1 = field(0, p, base), field(1, p, base)
                before = jnp.where(lane == 0, pltpu.roll(beside(1, p, r, 0), 1, 1), pltpu.roll(w1, 1, 1))
                after = jnp.where(
                    lane == T - 1, pltpu.roll(beside(0, p, r, 2), T - 1, 1), pltpu.roll(w0, T - 1, 1)
                )
                upper = e0 * w0 + h0 * w1 + h1 * field(1, p, base - 1) + h2 * before + acc[0, p, rows, :]
                lower = e1 * w1 + h0 * w0 + h1s * field(0, p, base + 1) + h2s * after + acc[1, p, rows, :]
                for a, value in enumerate((upper, lower)):
                    if first:
                        wide_out[layer, a, p, rows, :] = value
                    else:
                        value = 2.0 * value - prev[layer, a, p, rows, :]
                    narrow_out[r, layer, a * T : (a + 1) * T, p * T : (p + 1) * T] = value.astype(BF16)


def result_kernel(z_ref, part0, part1, part2, part3, out_one, out_two):
    z = z_ref[0, 0]
    for d, part in enumerate((part0, part1, part2, part3)):
        state = (z + RING - d) % RING
        for layer, out in enumerate((out_one, out_two)):
            for p in range(2):
                for a in range(2):
                    out[state, p, a] = part[layer, a * T : (a + 1) * T, p * T : (p + 1) * T].astype(F32)


SMEM = pl.BlockSpec(memory_space=pltpu.SMEM)
VMEM = pl.BlockSpec(memory_space=pltpu.VMEM)
PARAMS = pltpu.CompilerParams(vmem_limit_bytes=VMEM_LIMIT)


def step(first, last, idx, halo, bd1, bd2, ops, prev=None):
    wide = jax.ShapeDtypeStruct((2, 2, 2, RING * T, T), F32)
    narrow = jax.ShapeDtypeStruct((RING, 2, 2 * T, 2 * T), BF16)
    scratch = [
        pltpu.VMEM((3, 2, 2, HALO * T, T), F32),
        pltpu.VMEM((2, 2, HALO * T, T), F32),
        pltpu.VMEM((2 * T, 2 * T), BF16),
        pltpu.VMEM((2 * T, 2 * T), F32),
        pltpu.VMEM((2, 2, RING * T, T), F32),
        pltpu.VMEM((2, 2, RING * T, T), F32),
    ]
    if first:
        scratch.append(pltpu.VMEM((HOMES, 2 * T, 2 * T), BF16))
    operands = [idx, *halo, bd1, bd2, ops] + ([] if first else [prev])
    return pl.pallas_call(
        lambda *refs: step_kernel(first, last, *refs),
        out_shape=(wide, wide, narrow) if first else narrow,
        in_specs=[SMEM] + [VMEM] * (len(operands) - 1),
        out_specs=(VMEM, VMEM, VMEM) if first else VMEM,
        scratch_shapes=scratch,
        compiler_params=PARAMS,
    )(*operands)


def halo_of(region):
    top = moved(region[RING - 1], "gx", RING)
    bottom = moved(region[0], "gx", -RING)
    left = moved(region, "gy", 1)
    right = moved(region, "gy", -1)
    ends = jnp.stack([top, bottom])
    return (region, left, right, top, bottom, moved(ends, "gy", 1), moved(ends, "gy", -1))


def results(narrow, z, zs):
    parts = ring_scattered(narrow, z)
    shape = jax.ShapeDtypeStruct((RING, 2, 2, T, T), F32)
    return pl.pallas_call(
        result_kernel,
        out_shape=(shape, shape),
        in_specs=[SMEM] + [VMEM] * RING,
        out_specs=(VMEM, VMEM),
        compiler_params=PARAMS,
    )(zs, *parts)


def body(phase_one, phase_two, hop_one, hop_two, onsite_one, onsite_two, coupling, owner, target_row, live_strips):
    grid_row, grid_col = lax.axis_index("gx"), lax.axis_index("gy")
    rows_n, cols_n = lax.axis_size("gx"), lax.axis_size("gy")
    z = grid_row % RING
    zs = z.astype(jnp.int32).reshape(1, 1)

    strip = jnp.arange(KS, dtype=jnp.int32)
    active = strip < live_strips[0, 0]
    masked = jnp.where(active[:, None, None, None, None], coupling[0, 0], 0.0)
    weights = coded(masked.transpose(3, 4, 0, 1, 2).reshape(32, 256), COUPLING_UNIT)
    drow, dcol = owner[0, 0] // cols_n - grid_row, owner[0, 0] % cols_n - grid_col
    code = jnp.where(active, 1 + (drow + 1) * 3 + dcol + 1, 0)
    at = jnp.where(active, target_row[0, 0], 0)
    places = jnp.pad(jnp.stack([code, at]), ((0, 14), (0, 256 - KS))).astype(I16)
    small = jnp.concatenate([weights, places], 0)
    small = jnp.stack([moved(small, "gy", 1), small, moved(small, "gy", -1)])

    phases = coded(jnp.stack([phase_one, phase_two], 1), PHASE_UNIT)
    region = ordered(ring_scattered(phases, z), z)
    small = ordered(ring_gathered(small), z)
    small = jnp.concatenate(
        [moved(small[RING - 1 :], "gx", RING), small, moved(small[:1], "gx", -RING)], 0
    )

    hops = coded(jnp.stack([hop_one, hop_two]) - HOP_MID, HOP_UNIT)
    sites = coded(jnp.stack([onsite_one, onsite_two]), SITE_UNIT)
    row_after = moved(hops[:, 1, 0, :], "gx", -1)
    col_after = moved(hops[:, 2, :, 0], "gy", -1)
    edges = jnp.concatenate([row_after, col_after, jnp.zeros((12, T), I16)], 0)
    packed = jnp.concatenate([jnp.concatenate([hops, sites], 1).reshape(10 * T, T), edges], 0)
    operator_parts = ring_gathered(packed)

    halo = halo_of(region)

    small = small.reshape(HOMES, 48, 256)
    code = small[:, 32, :KS].astype(jnp.int32).reshape(HALO, 3, KS)
    at = small[:, 33, :KS].astype(jnp.int32).reshape(HALO, 3, KS)
    step_row = jnp.where(code > 0, (code - 1) // 3 - 1, 0)
    step_col = jnp.where(code > 0, (code - 1) % 3 - 1, 0)
    rb = jnp.arange(HALO, dtype=jnp.int32)[:, None, None] + step_row
    cb = jnp.arange(3, dtype=jnp.int32)[None, :, None] + step_col
    lands = (code > 0) & (cb == 1) & (rb >= 1) & (rb <= RING)
    land_row = jnp.where(lands, (rb - 1) * T + at, -1).reshape(HOMES * KS)
    any_land = jnp.any(lands, axis=2).astype(jnp.int32).reshape(HOMES)
    src_row = (rb * T + at)[1 : RING + 1, 1].reshape(RING * KS)
    src_col = jnp.broadcast_to(cb, (HALO, 3, KS))[1 : RING + 1, 1].reshape(RING * KS)
    inside = jnp.stack(
        [grid_row >= RING, grid_row < rows_n - RING, grid_col > 0, grid_col < cols_n - 1]
    ).astype(jnp.int32)
    idx = jnp.zeros((256,), jnp.int32)
    for start, values in ((0, land_row), (144, any_land), (164, src_row), (200, src_col), (240, inside)):
        idx = lax.dynamic_update_slice(idx, values, (start,))
    idx = idx.reshape(1, 256)

    bd1, bd2 = pl.pallas_call(
        build_kernel,
        out_shape=(
            jax.ShapeDtypeStruct((HOMES, 512, 256), BF16),
            jax.ShapeDtypeStruct((RING, 512, 256), BF16),
        ),
        in_specs=[VMEM],
        out_specs=(VMEM, VMEM),
        compiler_params=PARAMS,
    )(small)
    ops = pl.pallas_call(
        operators_kernel,
        out_shape=jax.ShapeDtypeStruct((2, 7, RING * T, T), F32),
        in_specs=[SMEM] + [VMEM] * RING,
        out_specs=VMEM,
        compiler_params=PARAMS,
    )(zs, *operator_parts)

    zero, one, one_narrow = step(True, False, idx, halo, bd1, bd2, ops)
    two_narrow = step(False, False, idx, halo_of(one_narrow), bd1, bd2, ops, zero)
    three_narrow = step(False, True, idx, halo_of(two_narrow), bd1, bd2, ops, one)
    two_a, two_b = results(two_narrow, z, zs)
    three_a, three_b = results(three_narrow, z, zs)
    return two_a, two_b, three_a, three_b


def solution(mesh):
    field = P(None, None, "gx", "gy")
    site = P(None, "gx", "gy")
    out = P(None, None, None, "gx", "gy")
    return jax.shard_map(
        body,
        mesh=mesh,
        in_specs=(
            field,
            field,
            site,
            site,
            site,
            site,
            P("gx", "gy", None, None, None, None, None),
            P("gx", "gy", None),
            P("gx", "gy", None),
            P("gx", "gy"),
        ),
        out_specs=(out, out, out, out),
        check_vma=False,
    )
```

```python
import math

import jax
import jax.numpy as jnp
from jax import lax
from jax.experimental import pallas as pl
from jax.experimental.pallas import tpu as pltpu
from jax.sharding import PartitionSpec as P

RING = 4
T = 128
KS = 8
SR = 16
HALO = RING + 2
HOMES = HALO * 3
F32 = jnp.float32
BF16 = jnp.bfloat16
I16 = jnp.int16
PHASE_UNIT = math.pi / 32768.0
HOP_MID, HOP_UNIT = 0.12, 0.04 / 32767.0
SITE_UNIT = 0.25 / 32767.0
COUPLING_UNIT = 0.3 / 32767.0
VMEM_LIMIT = 28 * 1024 * 1024


PHASE_ROWS = 4 * T
ROW_EDGE, COL_EDGE, CODE, AT = 64, 66, 68, 69
SMALL_ROWS = 80
CARGO = PHASE_ROWS + SMALL_ROWS
LAND, ANY, SRC_ROW, SRC_COL, USED = 0, 24, 48, 72, 96
IDX_ROWS = 120


def coded(values, unit):
    return jnp.clip(jnp.round(values * (1.0 / unit)), -32768.0, 32767.0).astype(jnp.int32).astype(I16)


def decoded(code):
    return code.astype(jnp.int32).astype(F32)


def moved(array, axis, by):
    size = lax.axis_size(axis)
    return lax.ppermute(array, axis, [(i, i + by) for i in range(size) if 0 <= i + by < size])


def ring_moved(array, by):
    size = lax.axis_size("gx")
    pairs = [(i, i // RING * RING + (i + by) % RING) for i in range(size)]
    return lax.ppermute(array, "gx", pairs)


def lane_iota(shape, dim):
    return lax.broadcasted_iota(jnp.int32, shape, dim)


def encode_kernel(flags, phase_one, phase_two, small, *outs):
    z = flags[0, 0]
    for d, out in enumerate(outs):
        state = (z + d) % RING
        for layer, phase in enumerate((phase_one, phase_two)):
            for a in range(2):
                at = (layer * 2 + a) * T
                out[at : at + T, :] = coded(phase[state, a], PHASE_UNIT)
        out[PHASE_ROWS:, :] = small[...]


def pack_kernel(hop_one, hop_two, onsite_one, onsite_two, out):
    for layer, (hop, site) in enumerate(((hop_one, onsite_one), (hop_two, onsite_two))):
        for n in range(5):
            at = (layer * 5 + n) * T
            value = coded(hop[n] - HOP_MID, HOP_UNIT) if n < 3 else coded(site[n - 3], SITE_UNIT)
            out[at : at + T, :] = value


def region_kernel(flags, part0, part1, part2, part3, region, first_block, last_block):
    z = flags[0, 0]
    for d, part in enumerate((part0, part1, part2, part3)):
        region[(z + RING - d) % RING] = part[...]
    first_block[...] = region[0]
    last_block[...] = region[RING - 1]


def operators_kernel(flags, part0, part1, part2, part3, ops):
    z = flags[0, 0]
    for d, part in enumerate((part0, part1, part2, part3)):
        at = pl.ds(pl.multiple_of((z + RING - d) % RING * T, T), T)
        for layer in range(2):
            for n in range(5):
                base = (layer * 5 + n) * T
                raw = decoded(part[base : base + T, :])
                ops[layer, n, at, :] = raw * HOP_UNIT + HOP_MID if n < 3 else raw * SITE_UNIT


def neighbourhood(own, left, right, top, bottom, lcorner, rcorner):
    def block(rb, cb):
        if 1 <= rb <= RING:
            return (left, own, right)[cb].at[rb - 1]
        if cb == 1:
            return top if rb == 0 else bottom
        return (lcorner if cb == 0 else rcorner).at[0 if rb == 0 else 1]

    return block


def build_kernel(own, left, right, top, bottom, lcorner, rcorner, ops_in, idx, bd1, bd2, ops, codes):
    block = neighbourhood(own, left, right, top, bottom, lcorner, rcorner)
    rows, cols = lane_iota((32, 256), 0), lane_iota((32, 256), 1)
    place = ((rows // 16 == cols // 128) & (rows % 16 == cols % 16)).astype(BF16)
    i, j = lane_iota((256, 256), 0), lane_iota((256, 256), 1)
    mask1 = (i // 32) == ((j // 16) % 8)
    mask2 = ((i // 16) % 8) == (j // 32)
    first = (((0,), (0,)), ((), ()))

    def spread(a, b, mask):
        full = lax.dot_general(a, b, first, preferred_element_type=F32)
        return jnp.where(mask, full, 0.0).astype(BF16)

    codes[...] = jnp.zeros_like(codes)
    for home in range(HOMES):
        rb, cb = divmod(home, 3)
        ref = block(rb, cb)
        c = jnp.concatenate([decoded(ref[PHASE_ROWS + n : PHASE_ROWS + n + 32, :]) for n in (0, 32)], 1)
        c = c * COUPLING_UNIT
        high = c.astype(BF16)
        low = (c - high.astype(F32)).astype(BF16)
        bd1[home, 0:256, :] = spread(high, place, mask1)
        bd1[home, 256:512, :] = spread(low, place, mask1)
        if cb == 1 and 1 <= rb <= RING:
            bd2[rb - 1, 0:256, :] = spread(place, high, mask2)
            bd2[rb - 1, 256:512, :] = spread(place, low, mask2)
        words = ref[PHASE_ROWS + 64 : PHASE_ROWS + 80, :].astype(jnp.int32)
        codes[0, home : home + 1, :] = words[CODE - 64 : CODE - 63, :]
        codes[1, home : home + 1, :] = words[AT - 64 : AT - 63, :]

    code, at = codes[0], codes[1]
    home = lane_iota((24, T), 0)
    active = code >= 16
    rb = home // 3 + jnp.where(active, ((code >> 2) & 3) - 1, 0)
    cb = home % 3 + jnp.where(active, (code & 3) - 1, 0)
    lands = active & (cb == 1) & (rb >= 1) & (rb <= RING)
    idx[LAND : LAND + 24, :] = jnp.where(lands, (rb - 1) * T + at, -1)
    some = jnp.max(jnp.where(lands, 1.0, 0.0), axis=1, keepdims=True)
    idx[ANY : ANY + 24, :] = jnp.broadcast_to(some, (24, T)).astype(jnp.int32)
    idx[SRC_ROW : SRC_ROW + 24, :] = jnp.clip(rb * T + at, 0, HALO * T - SR)
    idx[SRC_COL : SRC_COL + 24, :] = jnp.clip(cb, 0, 2)
    mine = active & (home % 3 == 1) & (home // 3 >= 1) & (home // 3 <= RING)
    source = jnp.where(mine, rb * 3 + cb, -1)
    idx[USED : USED + 24, :] = jnp.zeros((24, T), jnp.int32)
    for n in range(HOMES):
        hit = jnp.where(source == n, 1.0, 0.0)
        used = jnp.max(jnp.max(hit, axis=1, keepdims=True), axis=0, keepdims=True)
        idx[USED + n : USED + n + 1, :] = jnp.broadcast_to(used, (1, T)).astype(jnp.int32)

    ops[:, 0:5] = ops_in[...]
    lane = lane_iota((T, T), 1)

    def edge(ref, row):
        words = decoded(ref[PHASE_ROWS + 64 : PHASE_ROWS + 80, :])
        return words[row - 64 : row - 63, :] * HOP_UNIT + HOP_MID

    for layer in range(2):
        ops[layer, 5, 0 : RING * T - 1, :] = ops_in[layer, 1, 1 : RING * T, :]
        ops[layer, 5, RING * T - 1 : RING * T, :] = edge(bottom, ROW_EDGE + layer)
        for r in range(RING):
            rows = slice(r * T, (r + 1) * T)
            column = jnp.broadcast_to(edge(right.at[r], COL_EDGE + layer), (T, T)).T
            ops[layer, 6, rows, :] = jnp.where(lane == T - 1, column, pltpu.roll(ops_in[layer, 2, rows, :], T - 1, 1))


def cos_sin(code):
    q = code.astype(jnp.int32)
    quarter = (q + 8192) >> 14
    r = (q - (quarter << 14)).astype(F32) * PHASE_UNIT
    r2 = r * r
    s = r * (1.0 + r2 * (-1.6666654611e-1 + r2 * (8.3321608736e-3 + r2 * -1.9515295891e-4)))
    c = 1.0 + r2 * (-0.5 + r2 * (4.166664568298827e-2 + r2 * (-1.388731625493765e-3 + r2 * 2.443315711809948e-5)))
    odd = (quarter & 1) == 1
    cos_v = jnp.where(odd, s, c)
    sin_v = jnp.where(odd, c, s)
    cos_v = jnp.where(((quarter + 1) & 2) == 2, -cos_v, cos_v)
    sin_v = jnp.where((quarter & 2) == 2, -sin_v, sin_v)
    return cos_v, sin_v


def zero_kernel(region, zero_out, narrow_out):
    for rb in range(RING):
        rows = slice(rb * T, (rb + 1) * T)
        for layer in range(2):
            for a in range(2):
                at = (layer * 2 + a) * T
                pair = cos_sin(region[rb, at : at + T, :])
                for p in range(2):
                    zero_out[layer, a, p, rows, :] = pair[p]
                    narrow_out[rb, layer, a * T : (a + 1) * T, p * T : (p + 1) * T] = pair[p].astype(BF16)


def step_kernel(first, last, *refs):
    refs = list(refs)
    flags, idx, own, left, right, top, bottom, lcorner, rcorner, bd1, bd2, ops = refs[:12]
    refs = refs[12:]
    around = neighbourhood(own, left, right, top, bottom, lcorner, rcorner)
    prev = None if first else refs.pop(0)
    wide_out = refs.pop(0) if first else None
    if last:
        parts = refs[:RING]
        refs = refs[RING:]
        narrow_out = refs.pop()
    else:
        narrow_out, first_out, last_out = refs[:3]
        refs = refs[3:]
        parts = []
        if not first:
            parts = refs[:RING]
            refs = refs[RING:]
    fu, fv, gathered, terms, acc1, acc2 = refs[:6]
    xv = refs[6] if first else None

    def keep(rb, cb):
        if cb != 1:
            return flags[0, 3 if cb == 0 else 4].astype(F32)
        return flags[0, 1 if rb == 0 else 2].astype(F32)

    def store(layer, rb, cb, a, pair):
        for p in range(2):
            if layer == 1:
                xv[rb * 3 + cb, a * T : (a + 1) * T, p * T : (p + 1) * T] = pair[p]
            if layer == 0:
                fu[cb, a, p, rb * T : (rb + 1) * T, :] = pair[p].astype(F32)
            elif cb == 1:
                fv[a, p, rb * T : (rb + 1) * T, :] = pair[p].astype(F32)

    def decode(layer, rb, cb, a):
        at = (layer * 2 + a) * T
        pair = cos_sin(around(rb, cb)[at : at + T, :])
        factor = keep(rb, cb)
        store(layer, rb, cb, a, tuple((v * factor).astype(BF16) for v in pair))

    for cb in range(3):
        for rb in range(HALO):
            inner = 1 <= rb <= RING
            for layer in range(2):
                if first and not (cb == 1 and inner):
                    edge = None
                    if cb == 1:
                        edge = 1 if rb == 0 else 0
                    elif inner:
                        edge = 1 if cb == 0 else 0
                    if edge is not None:
                        decode(layer, rb, cb, edge)
                    home = rb * 3 + cb

                    @pl.when(idx[USED + home if layer == 0 else ANY + home, 0] > 0)
                    def _():
                        for a in range(2):
                            if a != edge:
                                decode(layer, rb, cb, a)

                    continue
                if layer == 1 and cb != 1:
                    continue
                ref = around(rb, cb).at[layer]
                for a in range(2):
                    for p in range(2):
                        value = ref[a * T : (a + 1) * T, p * T : (p + 1) * T].astype(F32)
                        if layer == 0:
                            fu[cb, a, p, rb * T : (rb + 1) * T, :] = value
                        else:
                            fv[a, p, rb * T : (rb + 1) * T, :] = value

    for r in range(RING):
        home = (r + 1) * 3 + 1
        for k in range(KS):
            row = idx[SRC_ROW + home, k]
            col = idx[SRC_COL + home, k]
            for a in range(2):
                for p in range(2):
                    piece = fu[col, a, p, pl.ds(row, SR), :].astype(BF16)
                    gathered[k * 32 + a * SR : k * 32 + (a + 1) * SR, p * T : (p + 1) * T] = piece
        both = jnp.dot(bd2[r], gathered[...], preferred_element_type=F32)
        summed = both[:256] + both[256:]
        for b in range(2):
            for p in range(2):
                acc2[b, p, r * T : (r + 1) * T, :] = summed[b * T : (b + 1) * T, p * T : (p + 1) * T]

    acc1[...] = jnp.zeros_like(acc1)
    for home in range(HOMES):
        rb, cb = divmod(home, 3)

        @pl.when(idx[ANY + home, 0] > 0)
        def _():
            decoded_here = first and not (cb == 1 and 1 <= rb <= RING)
            source = xv[home] if decoded_here else around(rb, cb)[1]
            both = jnp.dot(bd1[home], source, preferred_element_type=F32)
            terms[...] = both[:256] + both[256:]
            for k in range(KS):
                row = idx[LAND + home, k]

                @pl.when(row >= 0)
                def _():
                    for a in range(2):
                        for p in range(2):
                            at = (a, p, pl.ds(row, SR), slice(None))
                            acc1[at] = acc1[at] + terms[
                                k * 32 + a * SR : k * 32 + (a + 1) * SR, p * T : (p + 1) * T
                            ]

    lane = lane_iota((T, T), 1)
    for layer in range(2):
        acc = (acc1, acc2)[layer]

        def field(a, p, low):
            if layer == 0:
                return fu[1, a, p, low : low + T, :]
            return fv[a, p, low : low + T, :]

        def beside(a, p, r, cb):
            if layer == 0:
                return fu[cb, a, p, (r + 1) * T : (r + 2) * T, :]
            where = (slice(a * T, (a + 1) * T), slice(p * T, (p + 1) * T))
            if first:
                return xv[(r + 1) * 3 + cb, where[0], where[1]].astype(F32)
            return around(r + 1, cb)[1, where[0], where[1]].astype(F32)

        for r in range(RING):
            rows = slice(r * T, (r + 1) * T)
            h0, h1, h2, e0, e1, h1s, h2s = [ops[layer, n, rows, :] for n in range(7)]
            for p in range(2):
                base = (r + 1) * T
                w0, w1 = field(0, p, base), field(1, p, base)
                before = jnp.where(lane == 0, pltpu.roll(beside(1, p, r, 0), 1, 1), pltpu.roll(w1, 1, 1))
                after = jnp.where(
                    lane == T - 1, pltpu.roll(beside(0, p, r, 2), T - 1, 1), pltpu.roll(w0, T - 1, 1)
                )
                upper = e0 * w0 + h0 * w1 + h1 * field(1, p, base - 1) + h2 * before + acc[0, p, rows, :]
                lower = e1 * w1 + h0 * w0 + h1s * field(0, p, base + 1) + h2s * after + acc[1, p, rows, :]
                for a, value in enumerate((upper, lower)):
                    if first:
                        wide_out[layer, a, p, rows, :] = value
                    else:
                        value = 2.0 * value - prev[layer, a, p, rows, :]
                    narrow_out[r, layer, a * T : (a + 1) * T, p * T : (p + 1) * T] = value.astype(BF16)

    if not last:
        first_out[...] = narrow_out[0]
        last_out[...] = narrow_out[RING - 1]
    for d, part in enumerate(parts):
        part[...] = narrow_out[(flags[0, 0] + d) % RING]


def result_kernel(flags, part0, part1, part2, part3, out_one, out_two):
    z = flags[0, 0]
    for d, part in enumerate((part0, part1, part2, part3)):
        state = (z + RING - d) % RING
        for layer, out in enumerate((out_one, out_two)):
            for p in range(2):
                for a in range(2):
                    out[state, p, a] = part[layer, a * T : (a + 1) * T, p * T : (p + 1) * T].astype(F32)


SMEM = pl.BlockSpec(memory_space=pltpu.SMEM)
VMEM = pl.BlockSpec(memory_space=pltpu.VMEM)
PARAMS = pltpu.CompilerParams(vmem_limit_bytes=VMEM_LIMIT)
WIDE = jax.ShapeDtypeStruct((2, 2, 2, RING * T, T), F32)
NARROW = jax.ShapeDtypeStruct((RING, 2, 2 * T, 2 * T), BF16)
BLOCK = jax.ShapeDtypeStruct((2, 2 * T, 2 * T), BF16)


def local(kernel, out_shape, scalars, *operands, scratch=()):
    return pl.pallas_call(
        kernel,
        out_shape=out_shape,
        in_specs=[SMEM] * len(scalars) + [VMEM] * len(operands),
        out_specs=jax.tree.map(lambda _: VMEM, out_shape),
        scratch_shapes=list(scratch),
        compiler_params=PARAMS,
    )(*scalars, *operands)


def step(first, last, flags, idx, halo, bd1, bd2, ops, prev=None):
    scratch = [
        pltpu.VMEM((3, 2, 2, HALO * T, T), F32),
        pltpu.VMEM((2, 2, HALO * T, T), F32),
        pltpu.VMEM((2 * T, 2 * T), BF16),
        pltpu.VMEM((2 * T, 2 * T), F32),
        pltpu.VMEM((2, 2, RING * T, T), F32),
        pltpu.VMEM((2, 2, RING * T, T), F32),
    ]
    if first:
        scratch.append(pltpu.VMEM((HOMES, 2 * T, 2 * T), BF16))
        out = (WIDE, NARROW, BLOCK, BLOCK)
    elif last:
        scratch.append(pltpu.VMEM(NARROW.shape, BF16))
        out = (BLOCK,) * RING
    else:
        out = (NARROW, BLOCK, BLOCK) + (BLOCK,) * RING
    operands = [*halo, bd1, bd2, ops] + ([] if first else [prev])
    return local(lambda *refs: step_kernel(first, last, *refs), out, (flags, idx), *operands, scratch=scratch)


def halo_of(region, first_block, last_block):
    top = moved(last_block, "gx", RING)
    bottom = moved(first_block, "gx", -RING)
    left = moved(region, "gy", 1)
    right = moved(region, "gy", -1)
    ends = jnp.stack([top, bottom])
    return (region, left, right, top, bottom, moved(ends, "gy", 1), moved(ends, "gy", -1))


def results(flags, parts):
    parts = [parts[0]] + [ring_moved(parts[d], d) for d in range(1, RING)]
    shape = jax.ShapeDtypeStruct((RING, 2, 2, T, T), F32)
    return local(result_kernel, (shape, shape), (flags,), *parts)


def body(phase_one, phase_two, hop_one, hop_two, onsite_one, onsite_two, coupling, owner, target_row, live_strips):
    grid_row, grid_col = lax.axis_index("gx"), lax.axis_index("gy")
    rows_n, cols_n = lax.axis_size("gx"), lax.axis_size("gy")
    flags = jnp.stack(
        [grid_row % RING, grid_row >= RING, grid_row < rows_n - RING, grid_col > 0, grid_col < cols_n - 1]
    )
    flags = flags.astype(jnp.int32).reshape(1, 5)

    active = jnp.arange(KS, dtype=jnp.int32) < live_strips[0, 0]
    masked = jnp.where(active[:, None, None, None, None], coupling[0, 0], 0.0)
    weights = masked.reshape(2, 4, 2, SR, 2, SR).transpose(0, 4, 5, 1, 2, 3).reshape(64, T)
    drow, dcol = owner[0, 0] // cols_n - grid_row, owner[0, 0] % cols_n - grid_col
    code = jnp.where(active, 16 + (drow + 1) * 4 + dcol + 1, 0)
    at = jnp.where(active, target_row[0, 0], 0)
    places = jnp.pad(jnp.stack([code, at]), ((0, 10), (0, T - KS))).astype(I16)
    edges = jnp.stack([hop_one[1, 0, :], hop_two[1, 0, :], hop_one[2, :, 0], hop_two[2, :, 0]])
    small = jnp.concatenate([coded(weights, COUPLING_UNIT), coded(edges - HOP_MID, HOP_UNIT), places], 0)

    cargo = jax.ShapeDtypeStruct((CARGO, T), I16)
    sends = local(encode_kernel, (cargo,) * RING, (flags,), phase_one, phase_two, small)
    parts = [sends[0]] + [ring_moved(sends[d], d) for d in range(1, RING)]
    packed = local(
        pack_kernel, jax.ShapeDtypeStruct((10 * T, T), I16), (), hop_one, hop_two, onsite_one, onsite_two
    )
    packs = [packed] + [ring_moved(packed, d) for d in range(1, RING)]

    region = local(
        region_kernel, (jax.ShapeDtypeStruct((RING, CARGO, T), I16), cargo, cargo), (flags,), *parts
    )
    halo = halo_of(*region)
    zero, zero_narrow = local(zero_kernel, (WIDE, NARROW), (), region[0])
    ops = local(operators_kernel, jax.ShapeDtypeStruct((2, 5, RING * T, T), F32), (flags,), *packs)
    idx, bd1, bd2, ops = local(
        build_kernel,
        (
            jax.ShapeDtypeStruct((IDX_ROWS, T), jnp.int32),
            jax.ShapeDtypeStruct((HOMES, 512, 256), BF16),
            jax.ShapeDtypeStruct((RING, 512, 256), BF16),
            jax.ShapeDtypeStruct((2, 7, RING * T, T), F32),
        ),
        (),
        *halo,
        ops,
        scratch=[pltpu.VMEM((2, 24, T), jnp.int32)],
    )

    one, *one_blocks = step(True, False, flags, idx, (zero_narrow, *halo[1:]), bd1, bd2, ops)
    *two_blocks, part0, part1, part2, part3 = step(
        False, False, flags, idx, halo_of(*one_blocks), bd1, bd2, ops, zero
    )
    three_parts = step(False, True, flags, idx, halo_of(*two_blocks), bd1, bd2, ops, one)
    two_a, two_b = results(flags, (part0, part1, part2, part3))
    three_a, three_b = results(flags, three_parts)
    return two_a, two_b, three_a, three_b


def solution(mesh):
    field = P(None, None, "gx", "gy")
    site = P(None, "gx", "gy")
    out = P(None, None, None, "gx", "gy")
    return jax.shard_map(
        body,
        mesh=mesh,
        in_specs=(
            field,
            field,
            site,
            site,
            site,
            site,
            P("gx", "gy", None, None, None, None, None),
            P("gx", "gy", None),
            P("gx", "gy", None),
            P("gx", "gy"),
        ),
        out_specs=(out, out, out, out),
        check_vma=False,
    )
```

```python
import math

import jax
import jax.numpy as jnp
from jax import lax
from jax.experimental import pallas as pl
from jax.experimental.pallas import tpu as pltpu
from jax.sharding import PartitionSpec as P

RING = 4
T = 128
KS = 8
SR = 16
HALO = RING + 2
HOMES = HALO * 3
F32 = jnp.float32
BF16 = jnp.bfloat16
I16 = jnp.int16
PHASE_UNIT = math.pi / 32768.0
HOP_MID, HOP_UNIT = 0.12, 0.04 / 32767.0
SITE_UNIT = 0.25 / 32767.0
COUPLING_UNIT = 0.3 / 32767.0
VMEM_LIMIT = 28 * 1024 * 1024


PHASE_ROWS = 4 * T
ROW_EDGE, COL_EDGE, CODE, AT = 64, 66, 68, 69
SMALL_ROWS = 80
CARGO = PHASE_ROWS + SMALL_ROWS
LAND, ANY, SRC_ROW, SRC_COL, USED = 0, 24, 48, 72, 96
IDX_ROWS = 120


def coded(values, unit):
    return jnp.clip(jnp.round(values * (1.0 / unit)), -32768.0, 32767.0).astype(jnp.int32).astype(I16)


def decoded(code):
    return code.astype(jnp.int32).astype(F32)


def moved(array, axis, by):
    size = lax.axis_size(axis)
    return lax.ppermute(array, axis, [(i, i + by) for i in range(size) if 0 <= i + by < size])


def ring_moved(array, by):
    size = lax.axis_size("gx")
    pairs = [(i, i // RING * RING + (i + by) % RING) for i in range(size)]
    return lax.ppermute(array, "gx", pairs)


def lane_iota(shape, dim):
    return lax.broadcasted_iota(jnp.int32, shape, dim)


def started(copies, sems):
    copies = [pltpu.make_async_copy(source, to, sems.at[n]) for n, (source, to) in enumerate(copies)]
    for copy in copies:
        copy.start()
    return copies


def encode_kernel(flags, coupling, phase_one, phase_two, hop_one, hop_two, *refs):
    outs, (held, first_row, bonds, sems) = refs[:RING], refs[RING:]
    hops, phases = (hop_one, hop_two), (phase_one, phase_two)
    pending = started(
        [(hops[n].at[1, 0:8, :], first_row.at[n]) for n in range(2)]
        + [(hops[n].at[2], bonds.at[n]) for n in range(2)]
        + [(phases[n].at[(flags[0, 0] + d) % RING], held.at[d, n]) for d in range(RING) for n in range(2)],
        sems,
    )
    for copy in pending[:4]:
        copy.wait()
    live = flags[0, 8]
    lane = lane_iota((1, T), 1)
    code = jnp.zeros((1, T), jnp.int32)
    at = jnp.zeros((1, T), jnp.int32)
    for k in range(KS):
        owner, target = flags[0, 10 + k], flags[0, 10 + KS + k]
        strip = (owner // flags[0, 9] - flags[0, 5] + 1) * 4 + owner % flags[0, 9] - flags[0, 6] + 1
        here = (lane == k) & (k < live)
        code = jnp.where(here, strip + 16, code)
        at = jnp.where(here, target, at)
    weights = jnp.where(lane_iota((32, 256), 1) // 32 < live, coupling[...].T, 0.0)
    weights = coded(weights, COUPLING_UNIT)
    edges = [first_row[n, 0:1, :] for n in range(2)] + [bonds[n].T[0:1, :] for n in range(2)]
    edges = coded(jnp.concatenate(edges + [jnp.zeros((12, T), F32)], 0) - HOP_MID, HOP_UNIT).astype(jnp.int32)
    row = lane_iota((16, T), 0)
    words = jnp.where(row == CODE - 64, code, jnp.where(row == AT - 64, at, jnp.where(row < 4, edges, 0)))
    for d, out in enumerate(outs):
        for layer in range(2):
            pending[4 + d * 2 + layer].wait()
            for a in range(2):
                to = (layer * 2 + a) * T
                out[to : to + T, :] = coded(held[d, layer, a], PHASE_UNIT)
        out[PHASE_ROWS : PHASE_ROWS + 32, :] = weights[:, :T]
        out[PHASE_ROWS + 32 : PHASE_ROWS + 64, :] = weights[:, T:]
        out[PHASE_ROWS + 64 :, :] = words.astype(I16)


def pack_kernel(hop_one, hop_two, onsite_one, onsite_two, out, held, sems):
    fields = ((hop_one, onsite_one), (hop_two, onsite_two))
    pending = started(
        [
            (hop.at[n] if n < 3 else site.at[n - 3], held.at[layer, n])
            for layer, (hop, site) in enumerate(fields)
            for n in range(5)
        ],
        sems,
    )
    for layer in range(2):
        for n in range(5):
            at = layer * 5 + n
            pending[at].wait()
            value = held[layer, n]
            value = coded(value - HOP_MID, HOP_UNIT) if n < 3 else coded(value, SITE_UNIT)
            out[at * T : (at + 1) * T, :] = value


def region_kernel(flags, part0, part1, part2, part3, region, *edge_blocks):
    z = flags[0, 0]
    for d, part in enumerate((part0, part1, part2, part3)):
        region[(z + RING - d) % RING] = part[...]
    for slot in range(2):
        edge_blocks[slot][...] = region[edge_row(flags, slot) // (HALO - 1) * (RING - 1)]


def operators_kernel(flags, part0, part1, part2, part3, ops):
    z = flags[0, 0]
    for d, part in enumerate((part0, part1, part2, part3)):
        at = pl.ds(pl.multiple_of((z + RING - d) % RING * T, T), T)
        for layer in range(2):
            for n in range(5):
                base = (layer * 5 + n) * T
                raw = decoded(part[base : base + T, :])
                ops[layer, n, at, :] = raw * HOP_UNIT + HOP_MID if n < 3 else raw * SITE_UNIT


OWN, CROSS, NEAR = 0, 1, 2


def neighbourhood(own, ends, cross, cross_ends, near, near_ends):
    def block(row, side):
        if row in SLOTS:
            return (ends, cross_ends, near_ends)[side].at[SLOTS.index(row)]
        return (own, cross, near)[side].at[row - 1]

    return block


SLOTS = ("A", "B")
ROWS = (1, 2, 3, 4) + SLOTS


def edge_row(flags, slot):
    return flags[0, 7] if slot == 0 else HALO - 1 - flags[0, 7]


def row_of(flags, row):
    return edge_row(flags, SLOTS.index(row)) if row in SLOTS else row


def rows_of(rb):
    if isinstance(rb, int):
        return slice(rb * T, (rb + 1) * T)
    return pl.ds(pl.multiple_of(rb * T, T), T)


def column_of(flags, side):
    return 1 if side == OWN else flags[0, 3] if side == CROSS else 2 - flags[0, 3]


def build_kernel(flags, *refs):
    ops_in, idx, bd1, bd2, ops, codes = refs[6:]
    block = neighbourhood(*refs[:6])
    rows, cols = lane_iota((32, 256), 0), lane_iota((32, 256), 1)
    place = ((rows // 16 == cols // 128) & (rows % 16 == cols % 16)).astype(BF16)
    i, j = lane_iota((256, 256), 0), lane_iota((256, 256), 1)
    mask1 = (i // 32) == ((j // 16) % 8)
    mask2 = ((i // 16) % 8) == (j // 32)
    first = (((0,), (0,)), ((), ()))

    def spread(a, b, mask):
        full = lax.dot_general(a, b, first, preferred_element_type=F32)
        return jnp.where(mask, full, 0.0).astype(BF16)

    codes[...] = jnp.zeros_like(codes)
    for side in (OWN, CROSS, NEAR):
        for row in ROWS:
            home = row_of(flags, row) * 3 + column_of(flags, side)
            ref = block(row, side)
            c = jnp.concatenate([decoded(ref[PHASE_ROWS + n : PHASE_ROWS + n + 32, :]) for n in (0, 32)], 1)
            c = c * COUPLING_UNIT
            high = c.astype(BF16)
            low = (c - high.astype(F32)).astype(BF16)
            bd1[home, 0:256, :] = spread(high, place, mask1)
            bd1[home, 256:512, :] = spread(low, place, mask1)
            if side == OWN and row not in SLOTS:
                bd2[row - 1, 0:256, :] = spread(place, high, mask2)
                bd2[row - 1, 256:512, :] = spread(place, low, mask2)
            words = ref[PHASE_ROWS + 64 : PHASE_ROWS + 80, :].astype(jnp.int32)
            codes[0, pl.ds(home, 1), :] = words[CODE - 64 : CODE - 63, :]
            codes[1, pl.ds(home, 1), :] = words[AT - 64 : AT - 63, :]

    code, at = codes[0], codes[1]
    home = lane_iota((24, T), 0)
    active = code >= 16
    rb = home // 3 + jnp.where(active, ((code >> 2) & 3) - 1, 0)
    cb = home % 3 + jnp.where(active, (code & 3) - 1, 0)
    lands = active & (cb == 1) & (rb >= 1) & (rb <= RING)
    idx[LAND : LAND + 24, :] = jnp.where(lands, (rb - 1) * T + at, -1)
    some = jnp.max(jnp.where(lands, 1.0, 0.0), axis=1, keepdims=True)
    idx[ANY : ANY + 24, :] = jnp.broadcast_to(some, (24, T)).astype(jnp.int32)
    idx[SRC_ROW : SRC_ROW + 24, :] = jnp.clip(rb * T + at, 0, HALO * T - SR)
    idx[SRC_COL : SRC_COL + 24, :] = jnp.clip(cb, 0, 2)
    mine = active & (home % 3 == 1) & (home // 3 >= 1) & (home // 3 <= RING)
    source = jnp.where(mine, rb * 3 + cb, -1)
    idx[USED : USED + 24, :] = jnp.zeros((24, T), jnp.int32)
    for n in range(HOMES):
        hit = jnp.where(source == n, 1.0, 0.0)
        used = jnp.max(jnp.max(hit, axis=1, keepdims=True), axis=0, keepdims=True)
        idx[USED + n : USED + n + 1, :] = jnp.broadcast_to(used, (1, T)).astype(jnp.int32)

    ops[:, 0:5] = ops_in[...]
    lane = lane_iota((T, T), 1)

    def edge(ref, row):
        words = decoded(ref[PHASE_ROWS + 64 : PHASE_ROWS + 80, :])
        return words[row - 64 : row - 63, :] * HOP_UNIT + HOP_MID

    for layer in range(2):
        ops[layer, 5, 0 : RING * T - 1, :] = ops_in[layer, 1, 1 : RING * T, :]
        below = [edge(block(slot, OWN), ROW_EDGE + layer) for slot in SLOTS]
        ops[layer, 5, RING * T - 1 : RING * T, :] = jnp.where(
            jnp.broadcast_to(flags[0, 7], (1, T)) == HALO - 1, below[0], below[1]
        )
        for r in range(RING):
            rows = slice(r * T, (r + 1) * T)
            far, close = [edge(block(r + 1, side), COL_EDGE + layer) for side in (CROSS, NEAR)]
            right = jnp.where(jnp.broadcast_to(flags[0, 3], (1, T)) == 2, far, close)
            column = jnp.broadcast_to(right, (T, T)).T
            ops[layer, 6, rows, :] = jnp.where(lane == T - 1, column, pltpu.roll(ops_in[layer, 2, rows, :], T - 1, 1))


def cos_sin(code):
    q = code.astype(jnp.int32)
    quarter = (q + 8192) >> 14
    r = (q - (quarter << 14)).astype(F32) * PHASE_UNIT
    r2 = r * r
    s = r * (1.0 + r2 * (-1.6666654611e-1 + r2 * (8.3321608736e-3 + r2 * -1.9515295891e-4)))
    c = 1.0 + r2 * (-0.5 + r2 * (4.166664568298827e-2 + r2 * (-1.388731625493765e-3 + r2 * 2.443315711809948e-5)))
    odd = (quarter & 1) == 1
    cos_v = jnp.where(odd, s, c)
    sin_v = jnp.where(odd, c, s)
    cos_v = jnp.where(((quarter + 1) & 2) == 2, -cos_v, cos_v)
    sin_v = jnp.where((quarter & 2) == 2, -sin_v, sin_v)
    return cos_v, sin_v


def zero_kernel(region, zero_out, narrow_out):
    for rb in range(RING):
        rows = slice(rb * T, (rb + 1) * T)
        for layer in range(2):
            for a in range(2):
                at = (layer * 2 + a) * T
                pair = cos_sin(region[rb, at : at + T, :])
                for p in range(2):
                    zero_out[layer, a, p, rows, :] = pair[p]
                    narrow_out[rb, layer, a * T : (a + 1) * T, p * T : (p + 1) * T] = pair[p].astype(BF16)


def step_kernel(first, last, *refs):
    refs = list(refs)
    around = neighbourhood(*refs[2:8])
    flags, idx, bd1, bd2, ops = refs[:2] + refs[8:11]
    refs = refs[11:]
    prev = None if first else refs.pop(0)
    wide_out = refs.pop(0) if first else None
    if last:
        parts = refs[:RING]
        refs = refs[RING:]
        narrow_out = refs.pop()
    else:
        narrow_out, *edge_blocks = refs[:3]
        refs = refs[3:]
        parts = []
        if not first:
            parts = refs[:RING]
            refs = refs[RING:]
    fu, fv, fvs, gathered, terms, acc1, acc2 = refs[:7]
    xv = refs[7] if first else None

    def halves(p):
        return slice(p * T, (p + 1) * T)

    def decode(layer, row, side, a, edge):
        at = pl.multiple_of((layer * 2 + a) * T, T)
        pair = cos_sin(around(row, side)[pl.ds(at, T), :])
        if side == OWN:
            factor = flags[0, 1 + SLOTS.index(row)].astype(F32)
        else:
            factor = flags[0, 4].astype(F32) if side == CROSS else 1.0
        rb, cb = row_of(flags, row), column_of(flags, side)
        for p in range(2):
            value = (pair[p] * factor).astype(BF16)
            if layer == 0:
                fu[cb, a, p, rows_of(rb), :] = value.astype(F32)
                continue
            xv[rb * 3 + cb, pl.ds(pl.multiple_of(a * T, T), T), halves(p)] = value
            if side == OWN:
                fv[a, p, rows_of(rb), :] = value.astype(F32)
            elif edge:
                fvs[cb // 2, p, rows_of(rb - 1), :] = value.astype(F32)

    def widen(layer, row, side, a, edge):
        ref = around(row, side).at[layer]
        at = pl.ds(pl.multiple_of(a * T, T), T)
        rb, cb = row_of(flags, row), column_of(flags, side)
        for p in range(2):
            value = ref[at, halves(p)].astype(F32)
            if layer == 0:
                fu[cb, a, p, rows_of(rb), :] = value
            elif side == OWN:
                fv[a, p, rows_of(rb), :] = value
            elif edge:
                fvs[cb // 2, p, rows_of(rb - 1), :] = value

    for side, row in [(side, row) for side in (OWN, CROSS, NEAR) for row in ROWS]:
        cb = column_of(flags, side)
        for layer in range(2):
            if side == OWN and row not in SLOTS:
                for a in range(2):
                    widen(layer, row, side, a, False)
                continue
            edge = None
            if side == OWN:
                edge = 1 - row_of(flags, row) // (HALO - 1)
            elif row not in SLOTS:
                edge = 1 - cb // 2
            load = decode if first else widen
            if edge is not None:
                load(layer, row, side, edge, True)
            if layer == 1 and not first:
                continue

            @pl.when(idx[(USED if layer == 0 else ANY) + row_of(flags, row) * 3 + cb, 0] > 0)
            def _():
                for a in range(2) if edge is None else (1 - edge,):
                    load(layer, row, side, a, False)

    for r in range(RING):
        home = (r + 1) * 3 + 1
        for k in range(KS):
            row = idx[SRC_ROW + home, k]
            col = idx[SRC_COL + home, k]
            for a in range(2):
                for p in range(2):
                    piece = fu[col, a, p, pl.ds(row, SR), :].astype(BF16)
                    gathered[k * 32 + a * SR : k * 32 + (a + 1) * SR, p * T : (p + 1) * T] = piece
        both = jnp.dot(bd2[r], gathered[...], preferred_element_type=F32)
        summed = both[:256] + both[256:]
        for b in range(2):
            for p in range(2):
                acc2[b, p, r * T : (r + 1) * T, :] = summed[b * T : (b + 1) * T, p * T : (p + 1) * T]

    acc1[...] = jnp.zeros_like(acc1)
    for side, row in [(side, row) for side in (OWN, CROSS, NEAR) for row in ROWS]:
        home = row_of(flags, row) * 3 + column_of(flags, side)

        @pl.when(idx[ANY + home, 0] > 0)
        def _():
            decoded_here = first and (side != OWN or row in SLOTS)
            source = xv[home] if decoded_here else around(row, side)[1]
            both = jnp.dot(bd1[home], source, preferred_element_type=F32)
            terms[...] = both[:256] + both[256:]
            for k in range(KS):
                landing = idx[LAND + home, k]

                @pl.when(landing >= 0)
                def _():
                    for a in range(2):
                        for p in range(2):
                            at = (a, p, pl.ds(landing, SR), slice(None))
                            acc1[at] = acc1[at] + terms[
                                k * 32 + a * SR : k * 32 + (a + 1) * SR, p * T : (p + 1) * T
                            ]

    lane = lane_iota((T, T), 1)
    for layer in range(2):
        acc = (acc1, acc2)[layer]

        def field(a, p, low):
            if layer == 0:
                return fu[1, a, p, low : low + T, :]
            return fv[a, p, low : low + T, :]

        def beside(a, p, r, cb):
            if layer == 0:
                return fu[cb, a, p, (r + 1) * T : (r + 2) * T, :]
            return fvs[cb // 2, p, r * T : (r + 1) * T, :]

        for r in range(RING):
            rows = slice(r * T, (r + 1) * T)
            h0, h1, h2, e0, e1, h1s, h2s = [ops[layer, n, rows, :] for n in range(7)]
            for p in range(2):
                base = (r + 1) * T
                w0, w1 = field(0, p, base), field(1, p, base)
                before = jnp.where(lane == 0, pltpu.roll(beside(1, p, r, 0), 1, 1), pltpu.roll(w1, 1, 1))
                after = jnp.where(
                    lane == T - 1, pltpu.roll(beside(0, p, r, 2), T - 1, 1), pltpu.roll(w0, T - 1, 1)
                )
                upper = e0 * w0 + h0 * w1 + h1 * field(1, p, base - 1) + h2 * before + acc[0, p, rows, :]
                lower = e1 * w1 + h0 * w0 + h1s * field(0, p, base + 1) + h2s * after + acc[1, p, rows, :]
                for a, value in enumerate((upper, lower)):
                    if first:
                        wide_out[layer, a, p, rows, :] = value
                    else:
                        value = 2.0 * value - prev[layer, a, p, rows, :]
                    narrow_out[r, layer, a * T : (a + 1) * T, p * T : (p + 1) * T] = value.astype(BF16)

    if not last:
        for slot in range(2):
            edge_blocks[slot][...] = narrow_out[edge_row(flags, slot) // (HALO - 1) * (RING - 1)]
    for d, part in enumerate(parts):
        part[...] = narrow_out[(flags[0, 0] + d) % RING]


def result_kernel(shifts, flags, *refs):
    parts, refs = refs[: len(shifts)], refs[len(shifts) :]
    if shifts[0]:
        refs = refs[2:]
    outs, (held, sems) = refs[:2], refs[2:]
    pending = []
    for n, (d, part) in enumerate(zip(shifts, parts)):
        state = (flags[0, 0] + RING - d) % RING
        for layer, out in enumerate(outs):
            for p in range(2):
                for a in range(2):
                    value = part[layer, a * T : (a + 1) * T, p * T : (p + 1) * T]
                    held[n, layer, p, a] = value.astype(F32)
            copy = pltpu.make_async_copy(held.at[n, layer], out.at[state], sems.at[n * 2 + layer])
            copy.start()
            pending.append(copy)
    for copy in pending:
        copy.wait()


HBM = pl.BlockSpec(memory_space=pltpu.HBM)
SMEM = pl.BlockSpec(memory_space=pltpu.SMEM)
VMEM = pl.BlockSpec(memory_space=pltpu.VMEM)
PARAMS = pltpu.CompilerParams(vmem_limit_bytes=VMEM_LIMIT)
WIDE = jax.ShapeDtypeStruct((2, 2, 2, RING * T, T), F32)
NARROW = jax.ShapeDtypeStruct((RING, 2, 2 * T, 2 * T), BF16)
BLOCK = jax.ShapeDtypeStruct((2, 2 * T, 2 * T), BF16)


def local(kernel, out_shape, scalars, *operands, far=(), scratch=()):
    return pl.pallas_call(
        kernel,
        out_shape=out_shape,
        in_specs=[SMEM] * len(scalars) + [VMEM] * len(operands) + [HBM] * len(far),
        out_specs=jax.tree.map(lambda _: VMEM, out_shape),
        scratch_shapes=list(scratch),
        compiler_params=PARAMS,
    )(*scalars, *operands, *(pltpu.with_memory_space_constraint(x, pltpu.HBM) for x in far))


def step(first, last, flags, idx, halo, bd1, bd2, ops, prev=None):
    scratch = [
        pltpu.VMEM((3, 2, 2, HALO * T, T), F32),
        pltpu.VMEM((2, 2, HALO * T, T), F32),
        pltpu.VMEM((2, 2, RING * T, T), F32),
        pltpu.VMEM((2 * T, 2 * T), BF16),
        pltpu.VMEM((2 * T, 2 * T), F32),
        pltpu.VMEM((2, 2, RING * T, T), F32),
        pltpu.VMEM((2, 2, RING * T, T), F32),
    ]
    if first:
        scratch.append(pltpu.VMEM((HOMES, 2 * T, 2 * T), BF16))
        out = (WIDE, NARROW, BLOCK, BLOCK)
    elif last:
        scratch.append(pltpu.VMEM(NARROW.shape, BF16))
        out = (BLOCK,) * RING
    else:
        out = (NARROW, BLOCK, BLOCK) + (BLOCK,) * RING
    operands = [*halo, bd1, bd2, ops] + ([] if first else [prev])
    return local(lambda *refs: step_kernel(first, last, *refs), out, (flags, idx), *operands, scratch=scratch)


def across(array, low):
    size = lax.axis_size("gy")
    pairs = [(i, i + 1) for i in range(low, size - 1, 2)]
    return lax.ppermute(array, "gy", pairs + [(j, i) for i, j in pairs])


def swapped_rows(array, low):
    size = lax.axis_size("gx")
    pairs = [(i, i + RING) for i in range(size - RING) if i // RING % 2 == low]
    return lax.ppermute(array, "gx", pairs + [(j, i) for i, j in pairs])


def halo_of(region, block_a, block_b):
    cross, near = across(region, 1), across(region, 0)
    ends = jnp.stack([swapped_rows(block_a, 0), swapped_rows(block_b, 1)])
    return (region, ends, cross, across(ends, 1), near, across(ends, 0))


def ring_exchanged(parts):
    return [parts[0]] + [ring_moved(parts[d], d) for d in range(1, RING)]


def written(flags, shifts, parts, before=()):
    count = len(shifts)
    return pl.pallas_call(
        lambda *refs: result_kernel(shifts, *refs),
        out_shape=(jax.ShapeDtypeStruct((RING, 2, 2, T, T), F32),) * 2,
        in_specs=[SMEM] + [VMEM] * count + [HBM] * len(before),
        out_specs=(HBM, HBM),
        scratch_shapes=[pltpu.VMEM((count, 2, 2, 2, T, T), F32), pltpu.SemaphoreType.DMA((2 * count,))],
        input_output_aliases={1 + count + n: n for n in range(len(before))},
        compiler_params=PARAMS,
    )(flags, *parts, *before)


def results(flags, parts):
    own = written(flags, (0,), parts[:1])
    return written(flags, (1, 2, 3), parts[1:], own)


def body(phase_one, phase_two, hop_one, hop_two, onsite_one, onsite_two, coupling, owner, target_row, live_strips):
    grid_row, grid_col = lax.axis_index("gx"), lax.axis_index("gy")
    rows_n, cols_n = lax.axis_size("gx"), lax.axis_size("gy")
    odd, ring = grid_col % 2, grid_row // RING
    crossing = jnp.where(odd == 1, grid_col < cols_n - 1, grid_col > 0)
    second = jnp.where(ring % 2 == 1, ring < rows_n // RING - 1, ring > 0)
    first_row = jnp.where(ring % 2 == 1, 0, HALO - 1)
    flags = [grid_row % RING, ring // 2 * 2 + 1 < rows_n // RING, second, 2 * odd, crossing, grid_row, grid_col]
    flags += [first_row, live_strips[0, 0], cols_n]
    flags = [jnp.asarray(f).astype(jnp.int32).reshape(1) for f in flags]
    flags = jnp.concatenate(flags + [owner[0, 0], target_row[0, 0]]).reshape(1, 10 + 2 * KS)

    cargo = jax.ShapeDtypeStruct((CARGO, T), I16)
    sends = local(
        encode_kernel,
        (cargo,) * RING,
        (flags,),
        coupling.reshape(2 * KS * SR, 2 * SR),
        far=(phase_one, phase_two, hop_one, hop_two),
        scratch=[
            pltpu.VMEM((RING, 2, 2, T, T), F32),
            pltpu.VMEM((2, 8, T), F32),
            pltpu.VMEM((2, T, T), F32),
            pltpu.SemaphoreType.DMA((4 + 2 * RING,)),
        ],
    )
    parts = ring_exchanged(sends)
    packed = local(
        pack_kernel,
        jax.ShapeDtypeStruct((10 * T, T), I16),
        (),
        far=(hop_one, hop_two, onsite_one, onsite_two),
        scratch=[pltpu.VMEM((2, 5, T, T), F32), pltpu.SemaphoreType.DMA((10,))],
    )
    parts, packed = lax.optimization_barrier((parts, packed))
    packs = ring_exchanged([packed] * RING)

    region = local(
        region_kernel, (jax.ShapeDtypeStruct((RING, CARGO, T), I16), cargo, cargo), (flags,), *parts
    )
    halo = halo_of(*region)
    zero, zero_narrow = local(zero_kernel, (WIDE, NARROW), (), region[0])
    ops = local(operators_kernel, jax.ShapeDtypeStruct((2, 5, RING * T, T), F32), (flags,), *packs)
    idx, bd1, bd2, ops = local(
        build_kernel,
        (
            jax.ShapeDtypeStruct((IDX_ROWS, T), jnp.int32),
            jax.ShapeDtypeStruct((HOMES, 512, 256), BF16),
            jax.ShapeDtypeStruct((RING, 512, 256), BF16),
            jax.ShapeDtypeStruct((2, 7, RING * T, T), F32),
        ),
        (flags,),
        *halo,
        ops,
        scratch=[pltpu.VMEM((2, 24, T), jnp.int32)],
    )

    one, *one_blocks = step(True, False, flags, idx, (zero_narrow, *halo[1:]), bd1, bd2, ops)
    *two_blocks, part0, part1, part2, part3 = step(
        False, False, flags, idx, halo_of(*one_blocks), bd1, bd2, ops, zero
    )
    got1, got3 = ring_moved(part1, 1), ring_moved(part3, 3)
    halo, got1, got3, part2 = lax.optimization_barrier((halo_of(*two_blocks), got1, got3, part2))
    got2 = ring_moved(part2, 2)
    three_parts = step(False, True, flags, idx, halo, bd1, bd2, ops, one)
    three_parts, got2 = lax.optimization_barrier((three_parts, got2))
    two_a, two_b = results(flags, (part0, got1, got2, got3))
    three_a, three_b = results(flags, ring_exchanged(three_parts))
    return two_a, two_b, three_a, three_b


def solution(mesh):
    field = P(None, None, "gx", "gy")
    site = P(None, "gx", "gy")
    out = P(None, None, None, "gx", "gy")
    return jax.shard_map(
        body,
        mesh=mesh,
        in_specs=(
            field,
            field,
            site,
            site,
            site,
            site,
            P("gx", "gy", None, None, None, None, None),
            P("gx", "gy", None),
            P("gx", "gy", None),
            P("gx", "gy"),
        ),
        out_specs=(out, out, out, out),
        check_vma=False,
    )
```

```python
import functools
import math

import jax
import jax.numpy as jnp
from jax import lax
from jax.experimental import pallas as pl
from jax.experimental.pallas import tpu as pltpu
from jax.sharding import PartitionSpec as P

RING = 4
T = 128
KS = 8
SR = 16
HALO = RING + 2
HOMES = HALO * 3
F32 = jnp.float32
BF16 = jnp.bfloat16
I16 = jnp.int16
PHASE_UNIT = math.pi / 32768.0
HOP_MID, HOP_UNIT = 0.12, 0.04 / 32767.0
SITE_UNIT = 0.25 / 32767.0
COUPLING_UNIT = 0.3 / 32767.0
VMEM_LIMIT = 28 * 1024 * 1024


PHASE_ROWS = 4 * T
ROW_EDGE, COL_EDGE, CODE, AT = 64, 66, 68, 69
SMALL_ROWS = 80
CARGO = PHASE_ROWS + SMALL_ROWS
LAND, ANY, SRC_ROW, SRC_COL, USED = 0, 24, 48, 72, 96
IDX_ROWS = 120


def coded(values, unit):
    return jnp.clip(jnp.round(values * (1.0 / unit)), -32768.0, 32767.0).astype(jnp.int32).astype(I16)


def decoded(code):
    return code.astype(jnp.int32).astype(F32)


def moved(array, axis, by):
    size = lax.axis_size(axis)
    return lax.ppermute(array, axis, [(i, i + by) for i in range(size) if 0 <= i + by < size])


def ring_moved(array, by):
    size = lax.axis_size("gx")
    pairs = [(i, i // RING * RING + (i + by) % RING) for i in range(size)]
    return lax.ppermute(array, "gx", pairs)


def lane_iota(shape, dim):
    return lax.broadcasted_iota(jnp.int32, shape, dim)


def started(copies, sems):
    copies = [pltpu.make_async_copy(source, to, sems.at[n]) for n, (source, to) in enumerate(copies)]
    for copy in copies:
        copy.start()
    return copies


def encode_kernel(flags, coupling, phase_one, phase_two, hop_one, hop_two, *refs):
    outs, (held, first_row, bonds, sems) = refs[:RING], refs[RING:]
    hops, phases = (hop_one, hop_two), (phase_one, phase_two)
    pending = started(
        [(hops[n].at[1, 0:8, :], first_row.at[n]) for n in range(2)]
        + [(hops[n].at[2], bonds.at[n]) for n in range(2)]
        + [(phases[n].at[(flags[0, 0] + d) % RING], held.at[d, n]) for d in range(RING) for n in range(2)],
        sems,
    )
    for copy in pending[:4]:
        copy.wait()
    live = flags[0, 8]
    lane = lane_iota((1, T), 1)
    code = jnp.zeros((1, T), jnp.int32)
    at = jnp.zeros((1, T), jnp.int32)
    for k in range(KS):
        owner, target = flags[0, 10 + k], flags[0, 10 + KS + k]
        strip = (owner // flags[0, 9] - flags[0, 5] + 1) * 4 + owner % flags[0, 9] - flags[0, 6] + 1
        here = (lane == k) & (k < live)
        code = jnp.where(here, strip + 16, code)
        at = jnp.where(here, target, at)
    weights = jnp.where(lane_iota((32, 256), 1) // 32 < live, coupling[...].T, 0.0)
    weights = coded(weights, COUPLING_UNIT)
    edges = [first_row[n, 0:1, :] for n in range(2)] + [bonds[n].T[0:1, :] for n in range(2)]
    edges = coded(jnp.concatenate(edges + [jnp.zeros((12, T), F32)], 0) - HOP_MID, HOP_UNIT).astype(jnp.int32)
    row = lane_iota((16, T), 0)
    words = jnp.where(row == CODE - 64, code, jnp.where(row == AT - 64, at, jnp.where(row < 4, edges, 0)))
    for d, out in enumerate(outs):
        for layer in range(2):
            pending[4 + d * 2 + layer].wait()
            for a in range(2):
                to = (layer * 2 + a) * T
                out[to : to + T, :] = coded(held[d, layer, a], PHASE_UNIT)
        out[PHASE_ROWS : PHASE_ROWS + 32, :] = weights[:, :T]
        out[PHASE_ROWS + 32 : PHASE_ROWS + 64, :] = weights[:, T:]
        out[PHASE_ROWS + 64 :, :] = words.astype(I16)


def pack_kernel(hop_one, hop_two, onsite_one, onsite_two, out, held, sems):
    fields = ((hop_one, onsite_one), (hop_two, onsite_two))
    pending = started(
        [
            (hop.at[n] if n < 3 else site.at[n - 3], held.at[layer, n])
            for layer, (hop, site) in enumerate(fields)
            for n in range(5)
        ],
        sems,
    )
    for layer in range(2):
        for n in range(5):
            at = layer * 5 + n
            pending[at].wait()
            value = held[layer, n]
            value = coded(value - HOP_MID, HOP_UNIT) if n < 3 else coded(value, SITE_UNIT)
            out[at * T : (at + 1) * T, :] = value


def region_kernel(flags, part0, part1, part2, part3, region, *edge_blocks):
    z = flags[0, 0]
    for d, part in enumerate((part0, part1, part2, part3)):
        region[(z + RING - d) % RING] = part[...]
    for slot in range(2):
        edge_blocks[slot][...] = region[edge_row(flags, slot) // (HALO - 1) * (RING - 1)]


def operators_kernel(flags, own, other, far, ops):
    z = flags[0, 0]
    blocks = ((own, z), (other, z + 1 - z % 2 * 2), (far.at[0], 3 - z), (far.at[1], 2 + z % 2 * 2 - z))
    for part, place in blocks:
        at = pl.ds(pl.multiple_of(place * T, T), T)
        for layer in range(2):
            for n in range(5):
                base = (layer * 5 + n) * T
                raw = decoded(part[base : base + T, :])
                ops[layer, n, at, :] = raw * HOP_UNIT + HOP_MID if n < 3 else raw * SITE_UNIT


OWN, CROSS, NEAR = 0, 1, 2


def neighbourhood(own, ends, near, near_ends, cross, cross_ends):
    def block(row, side):
        if row in SLOTS:
            return (ends, cross_ends, near_ends)[side].at[SLOTS.index(row)]
        return (own, cross, near)[side].at[row - 1]

    return block


SLOTS = ("A", "B")
ROWS = (1, 2, 3, 4) + SLOTS


def edge_row(flags, slot):
    return flags[0, 7] if slot == 0 else HALO - 1 - flags[0, 7]


def row_of(flags, row):
    return edge_row(flags, SLOTS.index(row)) if row in SLOTS else row


def rows_of(rb):
    if isinstance(rb, int):
        return slice(rb * T, (rb + 1) * T)
    return pl.ds(pl.multiple_of(rb * T, T), T)


def column_of(flags, side):
    return 1 if side == OWN else flags[0, 3] if side == CROSS else 2 - flags[0, 3]


def coupling_tables(ref, home, bd1, bd2=None, n=None):
    rows, cols = lane_iota((32, 256), 0), lane_iota((32, 256), 1)
    place = ((rows // 16 == cols // 128) & (rows % 16 == cols % 16)).astype(BF16)
    i, j = lane_iota((256, 256), 0), lane_iota((256, 256), 1)
    mask1 = (i // 32) == ((j // 16) % 8)
    mask2 = ((i // 16) % 8) == (j // 32)
    first = (((0,), (0,)), ((), ()))

    def spread(a, b, mask):
        full = lax.dot_general(a, b, first, preferred_element_type=F32)
        return jnp.where(mask, full, 0.0).astype(BF16)

    c = jnp.concatenate([decoded(ref[PHASE_ROWS + m : PHASE_ROWS + m + 32, :]) for m in (0, 32)], 1)
    c = c * COUPLING_UNIT
    high = c.astype(BF16)
    low = (c - high.astype(F32)).astype(BF16)
    bd1[home, 0:256, :] = spread(high, place, mask1)
    bd1[home, 256:512, :] = spread(low, place, mask1)
    if bd2 is not None:
        bd2[n, 0:256, :] = spread(place, high, mask2)
        bd2[n, 256:512, :] = spread(place, low, mask2)


def build_kernel(flags, *refs):
    idx, bd1, ops, codes = refs[8:]
    block = neighbourhood(*refs[:6])
    codes[...] = jnp.zeros_like(codes)
    for side in (OWN, CROSS, NEAR):
        for row in ROWS:
            home = row_of(flags, row) * 3 + column_of(flags, side)
            ref = block(row, side)
            if side != OWN or row in SLOTS:
                coupling_tables(ref, home, bd1)
            words = ref[PHASE_ROWS + 64 : PHASE_ROWS + 80, :].astype(jnp.int32)
            codes[0, pl.ds(home, 1), :] = words[CODE - 64 : CODE - 63, :]
            codes[1, pl.ds(home, 1), :] = words[AT - 64 : AT - 63, :]

    code, at = codes[0], codes[1]
    home = lane_iota((24, T), 0)
    active = code >= 16
    rb = home // 3 + jnp.where(active, ((code >> 2) & 3) - 1, 0)
    cb = home % 3 + jnp.where(active, (code & 3) - 1, 0)
    lands = active & (cb == 1) & (rb >= 1) & (rb <= RING)
    idx[LAND : LAND + 24, :] = jnp.where(lands, (rb - 1) * T + at, -1)
    some = jnp.max(jnp.where(lands, 1.0, 0.0), axis=1, keepdims=True)
    idx[ANY : ANY + 24, :] = jnp.broadcast_to(some, (24, T)).astype(jnp.int32)
    idx[SRC_ROW : SRC_ROW + 24, :] = jnp.clip(rb * T + at, 0, HALO * T - SR)
    idx[SRC_COL : SRC_COL + 24, :] = jnp.clip(cb, 0, 2)
    mine = active & (home % 3 == 1) & (home // 3 >= 1) & (home // 3 <= RING)
    source = jnp.where(mine, rb * 3 + cb, -1)
    idx[USED : USED + 24, :] = jnp.zeros((24, T), jnp.int32)
    for n in range(HOMES):
        hit = jnp.where(source == n, 1.0, 0.0)
        used = jnp.max(jnp.max(hit, axis=1, keepdims=True), axis=0, keepdims=True)
        idx[USED + n : USED + n + 1, :] = jnp.broadcast_to(used, (1, T)).astype(jnp.int32)

    lane = lane_iota((T, T), 1)

    def edge(ref, row):
        words = decoded(ref[PHASE_ROWS + 64 : PHASE_ROWS + 80, :])
        return words[row - 64 : row - 63, :] * HOP_UNIT + HOP_MID

    for layer in range(2):
        ops[layer, 5, 0 : RING * T - 1, :] = ops[layer, 1, 1 : RING * T, :]
        below = [edge(block(slot, OWN), ROW_EDGE + layer) for slot in SLOTS]
        ops[layer, 5, RING * T - 1 : RING * T, :] = jnp.where(
            jnp.broadcast_to(flags[0, 7], (1, T)) == HALO - 1, below[0], below[1]
        )
        for r in range(RING):
            rows = slice(r * T, (r + 1) * T)
            far, close = [edge(block(r + 1, side), COL_EDGE + layer) for side in (CROSS, NEAR)]
            right = jnp.where(jnp.broadcast_to(flags[0, 3], (1, T)) == 2, far, close)
            column = jnp.broadcast_to(right, (T, T)).T
            ops[layer, 6, rows, :] = jnp.where(lane == T - 1, column, pltpu.roll(ops[layer, 2, rows, :], T - 1, 1))


def cos_sin(code):
    q = code.astype(jnp.int32)
    quarter = (q + 8192) >> 14
    r = (q - (quarter << 14)).astype(F32) * PHASE_UNIT
    r2 = r * r
    s = r * (1.0 + r2 * (-1.6666654611e-1 + r2 * (8.3321608736e-3 + r2 * -1.9515295891e-4)))
    c = 1.0 + r2 * (-0.5 + r2 * (4.166664568298827e-2 + r2 * (-1.388731625493765e-3 + r2 * 2.443315711809948e-5)))
    odd = (quarter & 1) == 1
    cos_v = jnp.where(odd, s, c)
    sin_v = jnp.where(odd, c, s)
    cos_v = jnp.where(((quarter + 1) & 2) == 2, -cos_v, cos_v)
    sin_v = jnp.where((quarter & 2) == 2, -sin_v, sin_v)
    return cos_v, sin_v


def zero_kernel(region, zero_out, narrow_out, bd1, bd2):
    for rb in range(RING):
        coupling_tables(region.at[rb], (rb + 1) * 3 + 1, bd1, bd2, rb)
        for layer in range(2):
            for a in range(2):
                at = (layer * 2 + a) * T
                pair = cos_sin(region[rb, at : at + T, :])
                for p in range(2):
                    zero_out[layer, a, p, rows_of(rb), :] = pair[p]
                    narrow_out[rb, layer, a * T : (a + 1) * T, p * T : (p + 1) * T] = pair[p].astype(BF16)


def step_kernel(first, last, begin, end, *refs):
    refs = list(refs)
    flags, idx = refs[:2]
    refs = refs[2:]
    own = ends = cross = cross_ends = near = near_ends = sums_in = sums_out = prev = wide_out = narrow_out = None
    if begin:
        own, ends, near, near_ends = refs[:4]
        refs = refs[4:]
    if end:
        cross, cross_ends = refs[:2]
        refs = refs[2:]
    around = neighbourhood(own, ends, near, near_ends, cross, cross_ends)
    bd1, bd2, ops = refs[:3]
    refs = refs[3:]
    sides = (OWN, NEAR) * begin + (CROSS,) * end
    far_column = column_of(flags, CROSS)
    here = [(begin and end) or (column_of(flags, CROSS if end else NEAR) == cb) for cb in (0, 2)]
    if end and not begin:
        sums_in = refs.pop(0)
    if end and not first:
        prev = refs.pop(0)
    if first:
        wide_out = refs.pop(0)
    edge_blocks, parts = [], []
    if not end:
        sums_out = refs.pop(0)
    elif last:
        parts = refs[:RING]
        refs = refs[RING:]
        narrow_out = refs.pop()
    else:
        narrow_out, *edge_blocks = refs[:3]
        refs = refs[3:]
        if not first:
            parts = refs[:RING]
            refs = refs[RING:]
    fu, fv, fvs, gathered, sources, terms_a, terms_b, acc1, acc2, homes, count = refs[:11]
    xv = refs[11] if first else None

    def halves(p):
        return slice(p * T, (p + 1) * T)

    def decode(layer, row, side, a, edge):
        at = pl.multiple_of((layer * 2 + a) * T, T)
        pair = cos_sin(around(row, side)[pl.ds(at, T), :])
        if side == OWN:
            factor = flags[0, 1 + SLOTS.index(row)].astype(F32)
        else:
            factor = flags[0, 4].astype(F32) if side == CROSS else 1.0
        rb, cb = row_of(flags, row), column_of(flags, side)
        for p in range(2):
            value = (pair[p] * factor).astype(BF16)
            if layer == 0:
                fu[cb, a, p, rows_of(rb), :] = value.astype(F32)
                continue
            xv[rb * 3 + cb, pl.ds(pl.multiple_of(a * T, T), T), halves(p)] = value
            if side == OWN:
                fv[a, p, rows_of(rb), :] = value.astype(F32)
            elif edge:
                fvs[cb // 2, p, rows_of(rb - 1), :] = value.astype(F32)

    def widen(layer, row, side, a, edge):
        ref = around(row, side).at[layer]
        at = pl.ds(pl.multiple_of(a * T, T), T)
        rb, cb = row_of(flags, row), column_of(flags, side)
        for p in range(2):
            value = ref[at, halves(p)].astype(F32)
            if layer == 0:
                fu[cb, a, p, rows_of(rb), :] = value
            elif side == OWN:
                fv[a, p, rows_of(rb), :] = value
            elif edge:
                fvs[cb // 2, p, rows_of(rb - 1), :] = value

    for side, row in [(side, row) for side in sides for row in ROWS]:
        cb = column_of(flags, side)
        for layer in range(2):
            if side == OWN and row not in SLOTS:
                for a in range(2):
                    widen(layer, row, side, a, False)
                continue
            edge = None
            if side == OWN:
                edge = 1 - row_of(flags, row) // (HALO - 1)
            elif row not in SLOTS:
                edge = 1 - cb // 2
            load = decode if first else widen
            if edge is not None:
                load(layer, row, side, edge, True)
            if layer == 1 and not first:
                continue

            @pl.when(idx[(USED if layer == 0 else ANY) + row_of(flags, row) * 3 + cb, 0] > 0)
            def _():
                for a in range(2) if edge is None else (1 - edge,):
                    load(layer, row, side, a, False)

    if sums_in is not None:
        acc1[:, :, 0 : RING * T, :] = sums_in[0]
        acc2[...] = sums_in[1]
    else:
        acc1[...] = jnp.zeros_like(acc1)
        acc2[...] = jnp.zeros_like(acc2)
    for r in range(RING):
        home = (r + 1) * 3 + 1
        columns = [idx[SRC_COL + home, k] for k in range(KS)]
        wanted = [(col == far_column) if end else (col != far_column) for col in columns]
        for k in range(KS):
            source = idx[SRC_ROW + home, k]
            for a in range(2):
                for p in range(2):
                    piece = fu[columns[k], a, p, pl.ds(source, SR), :]
                    if not (begin and end):
                        piece = jnp.where(wanted[k], piece, 0.0)
                    gathered[r, k * 32 + a * SR : k * 32 + (a + 1) * SR, halves(p)] = piece.astype(BF16)
    for r in range(RING):
        both = jnp.dot(bd2[r], gathered[r], preferred_element_type=F32)
        summed = both[:256] + both[256:]
        for b in range(2):
            for p in range(2):
                acc2[b, p, rows_of(r), :] += summed[b * T : (b + 1) * T, halves(p)]

    count[0] = 1
    homes[0] = HOMES
    for side, row in [(side, row) for side in sides for row in ROWS]:
        home = row_of(flags, row) * 3 + column_of(flags, side)

        @pl.when(idx[ANY + home, 0] > 0)
        def _():
            n = count[0]
            decoded_here = first and (side != OWN or row in SLOTS)
            sources[n] = xv[home] if decoded_here else around(row, side)[1]
            homes[n] = home
            count[0] = n + 1

    homes[count[0]] = HOMES

    def product(n):
        both = jnp.dot(bd1[jnp.minimum(homes[n], HOMES - 1)], sources[n], preferred_element_type=F32)
        return both[:256] + both[256:]

    def scatter(n, held):
        for k in range(KS):
            landing = idx[LAND + homes[n], k]
            landing = jnp.where(landing < 0, RING * T, landing)
            for a in range(2):
                for p in range(2):
                    at = (a, p, pl.ds(landing, SR), slice(None))
                    acc1[at] = acc1[at] + held[k * 32 + a * SR : k * 32 + (a + 1) * SR, halves(p)]

    def pair(j, carry):
        terms_a[...] = product(2 * j + 1)
        scatter(2 * j, terms_b)
        terms_b[...] = product(2 * j + 2)
        scatter(2 * j + 1, terms_a)
        return carry

    pairs = count[0] // 2
    lax.fori_loop(0, pairs, pair, 0)
    scatter(2 * pairs, terms_b)

    lane = lane_iota((T, T), 1)
    for layer in range(2):
        acc = (acc1, acc2)[layer]

        def field(a, p, low):
            if layer == 0:
                return fu[1, a, p, low : low + T, :]
            return fv[a, p, low : low + T, :]

        def beside(a, p, r, cb):
            if layer == 0:
                return fu[cb, a, p, (r + 1) * T : (r + 2) * T, :]
            return fvs[cb // 2, p, r * T : (r + 1) * T, :]

        for r in range(RING):
            rows = rows_of(r)
            h0, h1, h2, e0, e1, h1s, h2s = [ops[layer, n, rows, :] for n in range(7)]
            for p in range(2):
                upper, lower = acc[0, p, rows, :], acc[1, p, rows, :]
                before = jnp.where((lane == 0) & here[0], pltpu.roll(beside(1, p, r, 0), 1, 1), 0.0)
                after = jnp.where((lane == T - 1) & here[1], pltpu.roll(beside(0, p, r, 2), T - 1, 1), 0.0)
                if begin:
                    base = (r + 1) * T
                    w0, w1 = field(0, p, base), field(1, p, base)
                    upper = upper + (e0 * w0 + h0 * w1 + h1 * field(1, p, base - 1))
                    lower = lower + (e1 * w1 + h0 * w0 + h1s * field(0, p, base + 1))
                    before = jnp.where(lane == 0, before, pltpu.roll(w1, 1, 1))
                    after = jnp.where(lane == T - 1, after, pltpu.roll(w0, T - 1, 1))
                upper = upper + h2 * before
                lower = lower + h2s * after
                for a, value in enumerate((upper, lower)):
                    if not end:
                        sums_out[layer, a, p, rows, :] = value
                        continue
                    if first:
                        wide_out[layer, a, p, rows, :] = value
                    else:
                        value = 2.0 * value - prev[layer, a, p, rows, :]
                    narrow_out[r, layer, a * T : (a + 1) * T, halves(p)] = value.astype(BF16)

    if edge_blocks:
        for slot in range(2):
            edge_blocks[slot][...] = narrow_out[edge_row(flags, slot) // (HALO - 1) * (RING - 1)]
    for d, part in enumerate(parts):
        part[...] = narrow_out[(flags[0, 0] + d) % RING]


def result_kernel(shifts, flags, *refs):
    parts, refs = refs[: len(shifts)], refs[len(shifts) :]
    if shifts[0]:
        refs = refs[2:]
    outs, (held, sems) = refs[:2], refs[2:]
    pending = []
    for n, (d, part) in enumerate(zip(shifts, parts)):
        state = (flags[0, 0] + RING - d) % RING
        for layer, out in enumerate(outs):
            for p in range(2):
                for a in range(2):
                    value = part[layer, a * T : (a + 1) * T, p * T : (p + 1) * T]
                    held[n, layer, p, a] = value.astype(F32)
            copy = pltpu.make_async_copy(held.at[n, layer], out.at[state], sems.at[n * 2 + layer])
            copy.start()
            pending.append(copy)
    for copy in pending:
        copy.wait()


HBM = pl.BlockSpec(memory_space=pltpu.HBM)
SMEM = pl.BlockSpec(memory_space=pltpu.SMEM)
VMEM = pl.BlockSpec(memory_space=pltpu.VMEM)
PARAMS = pltpu.CompilerParams(vmem_limit_bytes=VMEM_LIMIT)
WIDE = jax.ShapeDtypeStruct((2, 2, 2, RING * T, T), F32)
NARROW = jax.ShapeDtypeStruct((RING, 2, 2 * T, 2 * T), BF16)
BLOCK = jax.ShapeDtypeStruct((2, 2 * T, 2 * T), BF16)


def local(kernel, out_shape, scalars, *operands, far=(), scratch=(), cost=None, alias=None):
    return pl.pallas_call(
        kernel,
        out_shape=out_shape,
        in_specs=[SMEM] * len(scalars) + [VMEM] * len(operands) + [HBM] * len(far),
        out_specs=jax.tree.map(lambda _: VMEM, out_shape),
        scratch_shapes=list(scratch),
        compiler_params=PARAMS,
        cost_estimate=cost,
        input_output_aliases=alias or {},
    )(*scalars, *operands, *(pltpu.with_memory_space_constraint(x, pltpu.HBM) for x in far))


def step(first, last, begin, end, flags, idx, halo, *rest):
    scratch = [
        pltpu.VMEM((3, 2, 2, HALO * T, T), F32),
        pltpu.VMEM((2, 2, HALO * T, T), F32),
        pltpu.VMEM((2, 2, RING * T, T), F32),
        pltpu.VMEM((RING, 2 * T, 2 * T), BF16),
        pltpu.VMEM((HOMES + 2, 2 * T, 2 * T), BF16),
        pltpu.VMEM((2 * T, 2 * T), F32),
        pltpu.VMEM((2 * T, 2 * T), F32),
        pltpu.VMEM((2, 2, RING * T + SR, T), F32),
        pltpu.VMEM((2, 2, RING * T, T), F32),
        pltpu.SMEM((HOMES + 2,), jnp.int32),
        pltpu.SMEM((1,), jnp.int32),
    ]
    if first:
        scratch.append(pltpu.VMEM((HOMES, 2 * T, 2 * T), BF16))
        out = (WIDE, NARROW, BLOCK, BLOCK)
    elif not end:
        out = WIDE
    elif last:
        scratch.append(pltpu.VMEM(NARROW.shape, BF16))
        out = (BLOCK,) * RING
    else:
        out = (NARROW, BLOCK, BLOCK) + (BLOCK,) * RING
    halo = halo[: 6 if end else 4][0 if begin else 4 :]
    kernel = functools.partial(step_kernel, first, last, begin, end)
    moved_bytes = sum(math.prod(x.shape) * x.dtype.itemsize for x in (*halo, *rest, *jax.tree.leaves(out)))
    products = 2 * (RING + HALO) * 512 * 256 * 256
    cost = pl.CostEstimate(flops=products, bytes_accessed=moved_bytes, transcendentals=0)
    return local(kernel, out, (flags, idx), *halo, *rest, scratch=scratch, cost=cost)


def halved_step(last, flags, idx, halo, tables, prev):
    sums = step(False, last, True, False, flags, idx, halo, *tables)
    return step(False, last, False, True, flags, idx, halo, *tables, sums, prev)


def across(array, low):
    size = lax.axis_size("gy")
    pairs = [(i, i + 1) for i in range(low, size - 1, 2)]
    return lax.ppermute(array, "gy", pairs + [(j, i) for i, j in pairs])


def swapped_rows(array, low):
    size = lax.axis_size("gx")
    pairs = [(i, i + RING) for i in range(size - RING) if i // RING % 2 == low]
    return lax.ppermute(array, "gx", pairs + [(j, i) for i, j in pairs])


def halo_of(region, block_a, block_b, beside=()):
    cross, near = across(region, 1), across(region, 0)
    ends = jnp.stack([swapped_rows(block_a, 0), swapped_rows(block_b, 1)])
    ends, beside = lax.optimization_barrier((ends, beside))
    return (region, ends, near, across(ends, 0), cross, across(ends, 1)), beside


def ring_swapped(array, partner):
    size = lax.axis_size("gx")
    pairs = [(i, i // RING * RING + partner[i % RING]) for i in range(size)]
    return lax.ppermute(array, "gx", pairs)


def ring_exchanged(parts):
    return [parts[0]] + [ring_moved(parts[d], d) for d in range(1, RING)]


def written(flags, shifts, parts, before=()):
    count = len(shifts)
    return pl.pallas_call(
        lambda *refs: result_kernel(shifts, *refs),
        out_shape=(jax.ShapeDtypeStruct((RING, 2, 2, T, T), F32),) * 2,
        in_specs=[SMEM] + [VMEM] * count + [HBM] * len(before),
        out_specs=(HBM, HBM),
        scratch_shapes=[pltpu.VMEM((count, 2, 2, 2, T, T), F32), pltpu.SemaphoreType.DMA((2 * count,))],
        input_output_aliases={1 + count + n: n for n in range(len(before))},
        compiler_params=PARAMS,
    )(flags, *parts, *before)


def results(flags, parts, groups):
    out = ()
    for shifts in groups:
        out = written(flags, shifts, [parts[d] for d in shifts], out)
    return out


def body(phase_one, phase_two, hop_one, hop_two, onsite_one, onsite_two, coupling, owner, target_row, live_strips):
    grid_row, grid_col = lax.axis_index("gx"), lax.axis_index("gy")
    rows_n, cols_n = lax.axis_size("gx"), lax.axis_size("gy")
    odd, ring = grid_col % 2, grid_row // RING
    crossing = jnp.where(odd == 1, grid_col < cols_n - 1, grid_col > 0)
    second = jnp.where(ring % 2 == 1, ring < rows_n // RING - 1, ring > 0)
    first_row = jnp.where(ring % 2 == 1, 0, HALO - 1)
    flags = [grid_row % RING, ring // 2 * 2 + 1 < rows_n // RING, second, 2 * odd, crossing, grid_row, grid_col]
    flags += [first_row, live_strips[0, 0], cols_n]
    flags = [jnp.asarray(f).astype(jnp.int32).reshape(1) for f in flags]
    flags = jnp.concatenate(flags + [owner[0, 0], target_row[0, 0]]).reshape(1, 10 + 2 * KS)

    cargo = jax.ShapeDtypeStruct((CARGO, T), I16)
    sends = local(
        encode_kernel,
        (cargo,) * RING,
        (flags,),
        coupling.reshape(2 * KS * SR, 2 * SR),
        far=(phase_one, phase_two, hop_one, hop_two),
        scratch=[
            pltpu.VMEM((RING, 2, 2, T, T), F32),
            pltpu.VMEM((2, 8, T), F32),
            pltpu.VMEM((2, T, T), F32),
            pltpu.SemaphoreType.DMA((4 + 2 * RING,)),
        ],
    )
    parts = ring_exchanged(sends)
    packed = local(
        pack_kernel,
        jax.ShapeDtypeStruct((10 * T, T), I16),
        (),
        far=(hop_one, hop_two, onsite_one, onsite_two),
        scratch=[pltpu.VMEM((2, 5, T, T), F32), pltpu.SemaphoreType.DMA((10,))],
    )
    other = ring_swapped(packed, (1, 0, 3, 2))
    parts, other = lax.optimization_barrier((parts, other))
    packs = (packed, other, ring_swapped(jnp.stack([packed, other]), (3, 2, 1, 0)))

    region = local(
        region_kernel, (jax.ShapeDtypeStruct((RING, CARGO, T), I16), cargo, cargo), (flags,), *parts
    )
    table = jax.ShapeDtypeStruct((HOMES, 512, 256), BF16)
    early = local(
        zero_kernel, (WIDE, NARROW, table, jax.ShapeDtypeStruct((RING, 512, 256), BF16)), (), region[0]
    )
    halo, (zero, zero_narrow, bd1, bd2) = halo_of(*region, early)
    ops_shape = jax.ShapeDtypeStruct((2, 7, RING * T, T), F32)
    ops = local(operators_kernel, ops_shape, (flags,), *packs)
    idx, bd1, ops = local(
        build_kernel,
        (jax.ShapeDtypeStruct((IDX_ROWS, T), jnp.int32), table, ops_shape),
        (flags,),
        *halo,
        bd1,
        ops,
        scratch=[pltpu.VMEM((2, 24, T), jnp.int32)],
        alias={7: 1, 8: 2},
    )

    tables = (bd1, bd2, ops)
    one, *one_blocks = step(True, False, True, True, flags, idx, (zero_narrow, *halo[1:]), *tables)
    *two_blocks, part0, part1, part2, part3 = halved_step(
        False, flags, idx, halo_of(*one_blocks)[0], tables, zero
    )
    got = ring_exchanged((part0, part1, part2, part3))
    three_parts = halved_step(True, flags, idx, halo_of(*two_blocks)[0], tables, one)
    three_parts, got = lax.optimization_barrier((three_parts, got))
    two_a, two_b = results(flags, got, ((0,), (1, 2, 3)))
    three_a, three_b = results(flags, ring_exchanged(three_parts), ((0,), (1,), (2,), (3,)))
    return two_a, two_b, three_a, three_b


def solution(mesh):
    field = P(None, None, "gx", "gy")
    site = P(None, "gx", "gy")
    out = P(None, None, None, "gx", "gy")
    return jax.shard_map(
        body,
        mesh=mesh,
        in_specs=(
            field,
            field,
            site,
            site,
            site,
            site,
            P("gx", "gy", None, None, None, None, None),
            P("gx", "gy", None),
            P("gx", "gy", None),
            P("gx", "gy"),
        ),
        out_specs=(out, out, out, out),
        check_vma=False,
    )
```

```python
import functools
import math

import jax
import jax.numpy as jnp
from jax import lax
from jax.experimental import pallas as pl
from jax.experimental.pallas import tpu as pltpu
from jax.sharding import PartitionSpec as P

RING = 4
T = 128
KS = 8
SR = 16
HALO = RING + 2
HOMES = HALO * 3
F32 = jnp.float32
BF16 = jnp.bfloat16
I16 = jnp.int16
PHASE_UNIT = math.pi / 32768.0
HOP_MID, HOP_UNIT = 0.12, 0.04 / 32767.0
SITE_UNIT = 0.25 / 32767.0
COUPLING_UNIT = 0.3 / 32767.0
VMEM_LIMIT = 28 * 1024 * 1024


PHASE_ROWS = 4 * T
ROW_EDGE, COL_EDGE, CODE, AT = 64, 66, 68, 69
SMALL_ROWS = 80
CARGO = PHASE_ROWS + SMALL_ROWS
LAND, ANY, SRC_ROW, SRC_COL, USED = 0, 24, 48, 72, 96
IDX_ROWS = 120


def coded(values, unit):
    return jnp.clip(jnp.round(values * (1.0 / unit)), -32768.0, 32767.0).astype(jnp.int32).astype(I16)


def decoded(code):
    return code.astype(jnp.int32).astype(F32)


def moved(array, axis, by):
    size = lax.axis_size(axis)
    return lax.ppermute(array, axis, [(i, i + by) for i in range(size) if 0 <= i + by < size])


def ring_moved(array, by):
    size = lax.axis_size("gx")
    pairs = [(i, i // RING * RING + (i + by) % RING) for i in range(size)]
    return lax.ppermute(array, "gx", pairs)


def lane_iota(shape, dim):
    return lax.broadcasted_iota(jnp.int32, shape, dim)


def started(copies, sems):
    copies = [pltpu.make_async_copy(source, to, sems.at[n]) for n, (source, to) in enumerate(copies)]
    for copy in copies:
        copy.start()
    return copies


def encode_kernel(flags, coupling, phase_one, phase_two, hop_one, hop_two, *refs):
    outs, (held, first_row, bonds, sems) = refs[:RING], refs[RING:]
    hops, phases = (hop_one, hop_two), (phase_one, phase_two)
    pending = started(
        [(hops[n].at[1, 0:8, :], first_row.at[n]) for n in range(2)]
        + [(hops[n].at[2], bonds.at[n]) for n in range(2)]
        + [(phases[n].at[(flags[0, 0] + d) % RING], held.at[d, n]) for d in range(RING) for n in range(2)],
        sems,
    )
    for copy in pending[:4]:
        copy.wait()
    live = flags[0, 8]
    lane = lane_iota((1, T), 1)
    code = jnp.zeros((1, T), jnp.int32)
    at = jnp.zeros((1, T), jnp.int32)
    for k in range(KS):
        owner, target = flags[0, 10 + k], flags[0, 10 + KS + k]
        strip = (owner // flags[0, 9] - flags[0, 5] + 1) * 4 + owner % flags[0, 9] - flags[0, 6] + 1
        here = (lane == k) & (k < live)
        code = jnp.where(here, strip + 16, code)
        at = jnp.where(here, target, at)
    weights = jnp.where(lane_iota((32, 256), 1) // 32 < live, coupling[...].T, 0.0)
    weights = coded(weights, COUPLING_UNIT)
    edges = [first_row[n, 0:1, :] for n in range(2)] + [bonds[n].T[0:1, :] for n in range(2)]
    edges = coded(jnp.concatenate(edges + [jnp.zeros((12, T), F32)], 0) - HOP_MID, HOP_UNIT).astype(jnp.int32)
    row = lane_iota((16, T), 0)
    words = jnp.where(row == CODE - 64, code, jnp.where(row == AT - 64, at, jnp.where(row < 4, edges, 0)))
    for d, out in enumerate(outs):
        for layer in range(2):
            pending[4 + d * 2 + layer].wait()
            for a in range(2):
                to = (layer * 2 + a) * T
                out[to : to + T, :] = coded(held[d, layer, a], PHASE_UNIT)
        out[PHASE_ROWS : PHASE_ROWS + 32, :] = weights[:, :T]
        out[PHASE_ROWS + 32 : PHASE_ROWS + 64, :] = weights[:, T:]
        out[PHASE_ROWS + 64 :, :] = words.astype(I16)


def pack_kernel(hop_one, hop_two, onsite_one, onsite_two, out, held, sems):
    fields = ((hop_one, onsite_one), (hop_two, onsite_two))
    pending = started(
        [
            (hop.at[n] if n < 3 else site.at[n - 3], held.at[layer, n])
            for layer, (hop, site) in enumerate(fields)
            for n in range(5)
        ],
        sems,
    )
    for layer in range(2):
        for n in range(5):
            at = layer * 5 + n
            pending[at].wait()
            value = held[layer, n]
            value = coded(value - HOP_MID, HOP_UNIT) if n < 3 else coded(value, SITE_UNIT)
            out[at * T : (at + 1) * T, :] = value


def region_kernel(flags, part0, part1, part2, part3, region, *edge_blocks):
    z = flags[0, 0]
    for d, part in enumerate((part0, part1, part2, part3)):
        region[(z + RING - d) % RING] = part[...]
    for slot in range(2):
        edge_blocks[slot][...] = region[edge_row(flags, slot) // (HALO - 1) * (RING - 1)]


def operators_kernel(flags, own, other, far, ops):
    z = flags[0, 0]
    blocks = ((own, z), (other, z + 1 - z % 2 * 2), (far.at[0], 3 - z), (far.at[1], 2 + z % 2 * 2 - z))
    for part, place in blocks:
        at = pl.ds(pl.multiple_of(place * T, T), T)
        for layer in range(2):
            for n in range(5):
                base = (layer * 5 + n) * T
                raw = decoded(part[base : base + T, :])
                ops[layer, n, at, :] = raw * HOP_UNIT + HOP_MID if n < 3 else raw * SITE_UNIT


OWN, CROSS, NEAR = 0, 1, 2


def neighbourhood(own, ends, near, near_ends, cross, cross_ends):
    def block(row, side):
        if row in SLOTS:
            return (ends, cross_ends, near_ends)[side].at[SLOTS.index(row)]
        return (own, cross, near)[side].at[row - 1]

    return block


SLOTS = ("A", "B")
ROWS = (1, 2, 3, 4) + SLOTS


def edge_row(flags, slot):
    return flags[0, 7] if slot == 0 else HALO - 1 - flags[0, 7]


def row_of(flags, row):
    return edge_row(flags, SLOTS.index(row)) if row in SLOTS else row


def rows_of(rb):
    if isinstance(rb, int):
        return slice(rb * T, (rb + 1) * T)
    return pl.ds(pl.multiple_of(rb * T, T), T)


def column_of(flags, side):
    return 1 if side == OWN else flags[0, 3] if side == CROSS else 2 - flags[0, 3]


def coupling_tables(ref, home, bd1, bd2=None, n=None):
    rows, cols = lane_iota((32, 256), 0), lane_iota((32, 256), 1)
    place = ((rows // 16 == cols // 128) & (rows % 16 == cols % 16)).astype(BF16)
    i, j = lane_iota((256, 256), 0), lane_iota((256, 256), 1)
    mask1 = (i // 32) == ((j // 16) % 8)
    mask2 = ((i // 16) % 8) == (j // 32)
    first = (((0,), (0,)), ((), ()))

    def spread(a, b, mask):
        full = lax.dot_general(a, b, first, preferred_element_type=F32)
        return jnp.where(mask, full, 0.0).astype(BF16)

    c = jnp.concatenate([decoded(ref[PHASE_ROWS + m : PHASE_ROWS + m + 32, :]) for m in (0, 32)], 1)
    c = c * COUPLING_UNIT
    high = c.astype(BF16)
    low = (c - high.astype(F32)).astype(BF16)
    bd1[home, 0:256, :] = spread(high, place, mask1)
    bd1[home, 256:512, :] = spread(low, place, mask1)
    if bd2 is not None:
        bd2[n, 0:256, :] = spread(place, high, mask2)
        bd2[n, 256:512, :] = spread(place, low, mask2)


def near_kernel(flags, own, ends, near, near_ends, bd1_in, ops_in, bd1, ops):
    block = neighbourhood(own, ends, near, near_ends, None, None)
    for side in (OWN, NEAR):
        for row in SLOTS if side == OWN else ROWS:
            coupling_tables(block(row, side), row_of(flags, row) * 3 + column_of(flags, side), bd1)
    lane = lane_iota((T, T), 1)
    for layer in range(2):
        ops[layer, 5, 0 : RING * T - 1, :] = ops[layer, 1, 1 : RING * T, :]
        below = [bond_edge(block(slot, OWN), ROW_EDGE + layer) for slot in SLOTS]
        ops[layer, 5, RING * T - 1 : RING * T, :] = jnp.where(
            jnp.broadcast_to(flags[0, 7], (1, T)) == HALO - 1, below[0], below[1]
        )
        for r in range(RING):
            column = jnp.broadcast_to(bond_edge(near.at[r], COL_EDGE + layer), (T, T)).T
            ops[layer, 6, rows_of(r), :] = jnp.where(
                lane == T - 1, column, pltpu.roll(ops[layer, 2, rows_of(r), :], T - 1, 1)
            )


def bond_edge(ref, row):
    words = decoded(ref[PHASE_ROWS + 64 : PHASE_ROWS + 80, :])
    return words[row - 64 : row - 63, :] * HOP_UNIT + HOP_MID


def cross_kernel(flags, *refs):
    idx, bd1, ops, codes = refs[8:]
    block = neighbourhood(*refs[:6])
    for row in ROWS:
        coupling_tables(block(row, CROSS), row_of(flags, row) * 3 + column_of(flags, CROSS), bd1)
    lane = lane_iota((T, T), 1)
    is_right = flags[0, 3] == 2
    for layer in range(2):
        for r in range(RING):
            column = jnp.broadcast_to(bond_edge(block(r + 1, CROSS), COL_EDGE + layer), (T, T)).T
            ops[layer, 6, rows_of(r), :] = jnp.where(
                (lane == T - 1) & is_right, column, ops[layer, 6, rows_of(r), :]
            )

    codes[...] = jnp.zeros_like(codes)
    for side in (OWN, CROSS, NEAR):
        for row in ROWS:
            home = row_of(flags, row) * 3 + column_of(flags, side)
            words = block(row, side)[PHASE_ROWS + 64 : PHASE_ROWS + 80, :].astype(jnp.int32)
            codes[0, pl.ds(home, 1), :] = words[CODE - 64 : CODE - 63, :]
            codes[1, pl.ds(home, 1), :] = words[AT - 64 : AT - 63, :]

    code, at = codes[0], codes[1]
    home = lane_iota((24, T), 0)
    active = code >= 16
    rb = home // 3 + jnp.where(active, ((code >> 2) & 3) - 1, 0)
    cb = home % 3 + jnp.where(active, (code & 3) - 1, 0)
    lands = active & (cb == 1) & (rb >= 1) & (rb <= RING)
    idx[LAND : LAND + 24, :] = jnp.where(lands, (rb - 1) * T + at, -1)
    some = jnp.max(jnp.where(lands, 1.0, 0.0), axis=1, keepdims=True)
    idx[ANY : ANY + 24, :] = jnp.broadcast_to(some, (24, T)).astype(jnp.int32)
    idx[SRC_ROW : SRC_ROW + 24, :] = jnp.clip(rb * T + at, 0, HALO * T - SR)
    idx[SRC_COL : SRC_COL + 24, :] = jnp.clip(cb, 0, 2)
    mine = active & (home % 3 == 1) & (home // 3 >= 1) & (home // 3 <= RING)
    source = jnp.where(mine, rb * 3 + cb, -1)
    idx[USED : USED + 24, :] = jnp.zeros((24, T), jnp.int32)
    for n in range(HOMES):
        hit = jnp.where(source == n, 1.0, 0.0)
        used = jnp.max(jnp.max(hit, axis=1, keepdims=True), axis=0, keepdims=True)
        idx[USED + n : USED + n + 1, :] = jnp.broadcast_to(used, (1, T)).astype(jnp.int32)


def cos_sin(code):
    q = code.astype(jnp.int32)
    quarter = (q + 8192) >> 14
    r = (q - (quarter << 14)).astype(F32) * PHASE_UNIT
    r2 = r * r
    s = r * (1.0 + r2 * (-1.6666654611e-1 + r2 * (8.3321608736e-3 + r2 * -1.9515295891e-4)))
    c = 1.0 + r2 * (-0.5 + r2 * (4.166664568298827e-2 + r2 * (-1.388731625493765e-3 + r2 * 2.443315711809948e-5)))
    odd = (quarter & 1) == 1
    cos_v = jnp.where(odd, s, c)
    sin_v = jnp.where(odd, c, s)
    cos_v = jnp.where(((quarter + 1) & 2) == 2, -cos_v, cos_v)
    sin_v = jnp.where((quarter & 2) == 2, -sin_v, sin_v)
    return cos_v, sin_v


def zero_kernel(region, zero_out, narrow_out, bd1, bd2):
    for rb in range(RING):
        coupling_tables(region.at[rb], (rb + 1) * 3 + 1, bd1, bd2, rb)
        for layer in range(2):
            for a in range(2):
                at = (layer * 2 + a) * T
                pair = cos_sin(region[rb, at : at + T, :])
                for p in range(2):
                    zero_out[layer, a, p, rows_of(rb), :] = pair[p]
                    narrow_out[rb, layer, a * T : (a + 1) * T, p * T : (p + 1) * T] = pair[p].astype(BF16)


def step_kernel(first, last, begin, end, *refs):
    refs = list(refs)
    flags, idx = refs[:2]
    refs = refs[2:]
    own = ends = cross = cross_ends = near = near_ends = sums_in = sums_out = prev = wide_out = narrow_out = None
    if begin:
        own, ends, near, near_ends = refs[:4]
        refs = refs[4:]
    if end:
        cross, cross_ends = refs[:2]
        refs = refs[2:]
    around = neighbourhood(own, ends, near, near_ends, cross, cross_ends)
    bd1, bd2, ops = refs[:3]
    refs = refs[3:]
    sides = (OWN, NEAR) * begin + (CROSS,) * end
    far_column = column_of(flags, CROSS)
    here = [(begin and end) or (column_of(flags, CROSS if end else NEAR) == cb) for cb in (0, 2)]
    if end and not begin:
        sums_in = refs.pop(0)
    if end and not first:
        prev = refs.pop(0)
    if first:
        wide_out = refs.pop(0)
    edge_blocks, parts = [], []
    if not end:
        sums_out = refs.pop(0)
    elif last:
        parts = refs[:RING]
        refs = refs[RING:]
        narrow_out = refs.pop()
    else:
        narrow_out, *edge_blocks = refs[:3]
        refs = refs[3:]
        if not first:
            parts = refs[:RING]
            refs = refs[RING:]
    fu, fv, fvs, gathered, sources, terms_a, terms_b, acc1, acc2, homes, count = refs[:11]
    xv = refs[11] if first else None

    def halves(p):
        return slice(p * T, (p + 1) * T)

    def decode(layer, row, side, a, edge):
        at = pl.multiple_of((layer * 2 + a) * T, T)
        pair = cos_sin(around(row, side)[pl.ds(at, T), :])
        if side == OWN:
            factor = flags[0, 1 + SLOTS.index(row)].astype(F32)
        else:
            factor = flags[0, 4].astype(F32) if side == CROSS else 1.0
        rb, cb = row_of(flags, row), column_of(flags, side)
        for p in range(2):
            value = (pair[p] * factor).astype(BF16)
            if layer == 0:
                fu[cb, a, p, rows_of(rb), :] = value.astype(F32)
                continue
            xv[rb * 3 + cb, pl.ds(pl.multiple_of(a * T, T), T), halves(p)] = value
            if side == OWN:
                fv[a, p, rows_of(rb), :] = value.astype(F32)
            elif edge:
                fvs[cb // 2, p, rows_of(rb - 1), :] = value.astype(F32)

    def widen(layer, row, side, a, edge):
        ref = around(row, side).at[layer]
        at = pl.ds(pl.multiple_of(a * T, T), T)
        rb, cb = row_of(flags, row), column_of(flags, side)
        for p in range(2):
            value = ref[at, halves(p)].astype(F32)
            if layer == 0:
                fu[cb, a, p, rows_of(rb), :] = value
            elif side == OWN:
                fv[a, p, rows_of(rb), :] = value
            elif edge:
                fvs[cb // 2, p, rows_of(rb - 1), :] = value

    for side, row in [(side, row) for side in sides for row in ROWS]:
        cb = column_of(flags, side)
        for layer in range(2):
            if side == OWN and row not in SLOTS:
                for a in range(2):
                    widen(layer, row, side, a, False)
                continue
            edge = None
            if side == OWN:
                edge = 1 - row_of(flags, row) // (HALO - 1)
            elif row not in SLOTS:
                edge = 1 - cb // 2
            load = decode if first else widen
            if edge is not None:
                load(layer, row, side, edge, True)
            if layer == 1 and not first:
                continue

            @pl.when(idx[(USED if layer == 0 else ANY) + row_of(flags, row) * 3 + cb, 0] > 0)
            def _():
                for a in range(2) if edge is None else (1 - edge,):
                    load(layer, row, side, a, False)

    if sums_in is not None:
        acc1[:, :, 0 : RING * T, :] = sums_in[0]
        acc2[...] = sums_in[1]
    else:
        acc1[...] = jnp.zeros_like(acc1)
        acc2[...] = jnp.zeros_like(acc2)
    for r in range(RING):
        home = (r + 1) * 3 + 1
        columns = [idx[SRC_COL + home, k] for k in range(KS)]
        wanted = [(col == far_column) if end else (col != far_column) for col in columns]
        for k in range(KS):
            source = idx[SRC_ROW + home, k]
            for a in range(2):
                for p in range(2):
                    piece = fu[columns[k], a, p, pl.ds(source, SR), :]
                    if not (begin and end):
                        piece = jnp.where(wanted[k], piece, 0.0)
                    gathered[r, k * 32 + a * SR : k * 32 + (a + 1) * SR, halves(p)] = piece.astype(BF16)
    for r in range(RING):
        both = jnp.dot(bd2[r], gathered[r], preferred_element_type=F32)
        summed = both[:256] + both[256:]
        for b in range(2):
            for p in range(2):
                acc2[b, p, rows_of(r), :] += summed[b * T : (b + 1) * T, halves(p)]

    count[0] = 1
    homes[0] = HOMES
    for side, row in [(side, row) for side in sides for row in ROWS]:
        home = row_of(flags, row) * 3 + column_of(flags, side)

        @pl.when(idx[ANY + home, 0] > 0)
        def _():
            n = count[0]
            decoded_here = first and (side != OWN or row in SLOTS)
            sources[n] = xv[home] if decoded_here else around(row, side)[1]
            homes[n] = home
            count[0] = n + 1

    homes[count[0]] = HOMES

    def product(n):
        both = jnp.dot(bd1[jnp.minimum(homes[n], HOMES - 1)], sources[n], preferred_element_type=F32)
        return both[:256] + both[256:]

    def scatter(n, held):
        for k in range(KS):
            landing = idx[LAND + homes[n], k]
            landing = jnp.where(landing < 0, RING * T, landing)
            for a in range(2):
                for p in range(2):
                    at = (a, p, pl.ds(landing, SR), slice(None))
                    acc1[at] = acc1[at] + held[k * 32 + a * SR : k * 32 + (a + 1) * SR, halves(p)]

    def pair(j, carry):
        terms_a[...] = product(2 * j + 1)
        scatter(2 * j, terms_b)
        terms_b[...] = product(2 * j + 2)
        scatter(2 * j + 1, terms_a)
        return carry

    pairs = count[0] // 2
    lax.fori_loop(0, pairs, pair, 0)
    scatter(2 * pairs, terms_b)

    lane = lane_iota((T, T), 1)
    for layer in range(2):
        acc = (acc1, acc2)[layer]

        def field(a, p, low):
            if layer == 0:
                return fu[1, a, p, low : low + T, :]
            return fv[a, p, low : low + T, :]

        def beside(a, p, r, cb):
            if layer == 0:
                return fu[cb, a, p, (r + 1) * T : (r + 2) * T, :]
            return fvs[cb // 2, p, r * T : (r + 1) * T, :]

        for r in range(RING):
            rows = rows_of(r)
            h0, h1, h2, e0, e1, h1s, h2s = [ops[layer, n, rows, :] for n in range(7)]
            for p in range(2):
                upper, lower = acc[0, p, rows, :], acc[1, p, rows, :]
                before = jnp.where((lane == 0) & here[0], pltpu.roll(beside(1, p, r, 0), 1, 1), 0.0)
                after = jnp.where((lane == T - 1) & here[1], pltpu.roll(beside(0, p, r, 2), T - 1, 1), 0.0)
                if begin:
                    base = (r + 1) * T
                    w0, w1 = field(0, p, base), field(1, p, base)
                    upper = upper + (e0 * w0 + h0 * w1 + h1 * field(1, p, base - 1))
                    lower = lower + (e1 * w1 + h0 * w0 + h1s * field(0, p, base + 1))
                    before = jnp.where(lane == 0, before, pltpu.roll(w1, 1, 1))
                    after = jnp.where(lane == T - 1, after, pltpu.roll(w0, T - 1, 1))
                upper = upper + h2 * before
                lower = lower + h2s * after
                for a, value in enumerate((upper, lower)):
                    if not end:
                        sums_out[layer, a, p, rows, :] = value
                        continue
                    if first:
                        wide_out[layer, a, p, rows, :] = value
                    else:
                        value = 2.0 * value - prev[layer, a, p, rows, :]
                    narrow_out[r, layer, a * T : (a + 1) * T, halves(p)] = value.astype(BF16)

    if edge_blocks:
        for slot in range(2):
            edge_blocks[slot][...] = narrow_out[edge_row(flags, slot) // (HALO - 1) * (RING - 1)]
    for d, part in enumerate(parts):
        part[...] = narrow_out[(flags[0, 0] + d) % RING]


def result_kernel(shifts, flags, *refs):
    parts, refs = refs[: len(shifts)], refs[len(shifts) :]
    if shifts[0]:
        refs = refs[2:]
    outs, (held, sems) = refs[:2], refs[2:]
    pending = []
    for n, (d, part) in enumerate(zip(shifts, parts)):
        state = (flags[0, 0] + RING - d) % RING
        for layer, out in enumerate(outs):
            for p in range(2):
                for a in range(2):
                    value = part[layer, a * T : (a + 1) * T, p * T : (p + 1) * T]
                    held[n, layer, p, a] = value.astype(F32)
            copy = pltpu.make_async_copy(held.at[n, layer], out.at[state], sems.at[n * 2 + layer])
            copy.start()
            pending.append(copy)
    for copy in pending:
        copy.wait()


HBM = pl.BlockSpec(memory_space=pltpu.HBM)
SMEM = pl.BlockSpec(memory_space=pltpu.SMEM)
VMEM = pl.BlockSpec(memory_space=pltpu.VMEM)
PARAMS = pltpu.CompilerParams(vmem_limit_bytes=VMEM_LIMIT)
WIDE = jax.ShapeDtypeStruct((2, 2, 2, RING * T, T), F32)
NARROW = jax.ShapeDtypeStruct((RING, 2, 2 * T, 2 * T), BF16)
BLOCK = jax.ShapeDtypeStruct((2, 2 * T, 2 * T), BF16)


def local(kernel, out_shape, scalars, *operands, far=(), scratch=(), cost=None, alias=None):
    return pl.pallas_call(
        kernel,
        out_shape=out_shape,
        in_specs=[SMEM] * len(scalars) + [VMEM] * len(operands) + [HBM] * len(far),
        out_specs=jax.tree.map(lambda _: VMEM, out_shape),
        scratch_shapes=list(scratch),
        compiler_params=PARAMS,
        cost_estimate=cost,
        input_output_aliases=alias or {},
    )(*scalars, *operands, *(pltpu.with_memory_space_constraint(x, pltpu.HBM) for x in far))


def step(first, last, begin, end, flags, idx, halo, *rest):
    scratch = [
        pltpu.VMEM((3, 2, 2, HALO * T, T), F32),
        pltpu.VMEM((2, 2, HALO * T, T), F32),
        pltpu.VMEM((2, 2, RING * T, T), F32),
        pltpu.VMEM((RING, 2 * T, 2 * T), BF16),
        pltpu.VMEM((HOMES + 2, 2 * T, 2 * T), BF16),
        pltpu.VMEM((2 * T, 2 * T), F32),
        pltpu.VMEM((2 * T, 2 * T), F32),
        pltpu.VMEM((2, 2, RING * T + SR, T), F32),
        pltpu.VMEM((2, 2, RING * T, T), F32),
        pltpu.SMEM((HOMES + 2,), jnp.int32),
        pltpu.SMEM((1,), jnp.int32),
    ]
    if first:
        scratch.append(pltpu.VMEM((HOMES, 2 * T, 2 * T), BF16))
        out = (WIDE, NARROW, BLOCK, BLOCK)
    elif not end:
        out = WIDE
    elif last:
        scratch.append(pltpu.VMEM(NARROW.shape, BF16))
        out = (BLOCK,) * RING
    else:
        out = (NARROW, BLOCK, BLOCK) + (BLOCK,) * RING
    halo = halo[: 6 if end else 4][0 if begin else 4 :]
    kernel = functools.partial(step_kernel, first, last, begin, end)
    moved_bytes = sum(math.prod(x.shape) * x.dtype.itemsize for x in (*halo, *rest, *jax.tree.leaves(out)))
    products = 2 * (RING + HALO) * 512 * 256 * 256
    cost = pl.CostEstimate(flops=products, bytes_accessed=moved_bytes, transcendentals=0)
    return local(kernel, out, (flags, idx), *halo, *rest, scratch=scratch, cost=cost)


def halved_step(last, flags, idx, halo, tables, prev):
    sums = step(False, last, True, False, flags, idx, halo, *tables)
    return step(False, last, False, True, flags, idx, halo, *tables, sums, prev)


def across(array, low):
    size = lax.axis_size("gy")
    pairs = [(i, i + 1) for i in range(low, size - 1, 2)]
    return lax.ppermute(array, "gy", pairs + [(j, i) for i, j in pairs])


def swapped_rows(array, low):
    size = lax.axis_size("gx")
    pairs = [(i, i + RING) for i in range(size - RING) if i // RING % 2 == low]
    return lax.ppermute(array, "gx", pairs + [(j, i) for i, j in pairs])


def halo_of(region, block_a, block_b, beside=()):
    cross, near = across(region, 1), across(region, 0)
    ends = jnp.stack([swapped_rows(block_a, 0), swapped_rows(block_b, 1)])
    ends, beside = lax.optimization_barrier((ends, beside))
    return (region, ends, near, across(ends, 0), cross, across(ends, 1)), beside


def ring_swapped(array, partner):
    size = lax.axis_size("gx")
    pairs = [(i, i // RING * RING + partner[i % RING]) for i in range(size)]
    return lax.ppermute(array, "gx", pairs)


def ring_exchanged(parts):
    return [parts[0]] + [ring_moved(parts[d], d) for d in range(1, RING)]


def written(flags, shifts, parts, before=()):
    count = len(shifts)
    return pl.pallas_call(
        lambda *refs: result_kernel(shifts, *refs),
        out_shape=(jax.ShapeDtypeStruct((RING, 2, 2, T, T), F32),) * 2,
        in_specs=[SMEM] + [VMEM] * count + [HBM] * len(before),
        out_specs=(HBM, HBM),
        scratch_shapes=[pltpu.VMEM((count, 2, 2, 2, T, T), F32), pltpu.SemaphoreType.DMA((2 * count,))],
        input_output_aliases={1 + count + n: n for n in range(len(before))},
        compiler_params=PARAMS,
    )(flags, *parts, *before)


def results(flags, parts, groups):
    out = ()
    for shifts in groups:
        out = written(flags, shifts, [parts[d] for d in shifts], out)
    return out


def body(phase_one, phase_two, hop_one, hop_two, onsite_one, onsite_two, coupling, owner, target_row, live_strips):
    grid_row, grid_col = lax.axis_index("gx"), lax.axis_index("gy")
    rows_n, cols_n = lax.axis_size("gx"), lax.axis_size("gy")
    odd, ring = grid_col % 2, grid_row // RING
    crossing = jnp.where(odd == 1, grid_col < cols_n - 1, grid_col > 0)
    second = jnp.where(ring % 2 == 1, ring < rows_n // RING - 1, ring > 0)
    first_row = jnp.where(ring % 2 == 1, 0, HALO - 1)
    flags = [grid_row % RING, ring // 2 * 2 + 1 < rows_n // RING, second, 2 * odd, crossing, grid_row, grid_col]
    flags += [first_row, live_strips[0, 0], cols_n]
    flags = [jnp.asarray(f).astype(jnp.int32).reshape(1) for f in flags]
    flags = jnp.concatenate(flags + [owner[0, 0], target_row[0, 0]]).reshape(1, 10 + 2 * KS)

    cargo = jax.ShapeDtypeStruct((CARGO, T), I16)
    sends = local(
        encode_kernel,
        (cargo,) * RING,
        (flags,),
        coupling.reshape(2 * KS * SR, 2 * SR),
        far=(phase_one, phase_two, hop_one, hop_two),
        scratch=[
            pltpu.VMEM((RING, 2, 2, T, T), F32),
            pltpu.VMEM((2, 8, T), F32),
            pltpu.VMEM((2, T, T), F32),
            pltpu.SemaphoreType.DMA((4 + 2 * RING,)),
        ],
    )
    parts = ring_exchanged(sends)
    packed = local(
        pack_kernel,
        jax.ShapeDtypeStruct((10 * T, T), I16),
        (),
        far=(hop_one, hop_two, onsite_one, onsite_two),
        scratch=[pltpu.VMEM((2, 5, T, T), F32), pltpu.SemaphoreType.DMA((10,))],
    )
    other = ring_swapped(packed, (1, 0, 3, 2))
    parts, other = lax.optimization_barrier((parts, other))

    region = local(
        region_kernel, (jax.ShapeDtypeStruct((RING, CARGO, T), I16), cargo, cargo), (flags,), *parts
    )
    region, both = lax.optimization_barrier((region, jnp.stack([packed, other])))
    packs = (packed, other, ring_swapped(both, (3, 2, 1, 0)))
    table = jax.ShapeDtypeStruct((HOMES, 512, 256), BF16)
    early = local(
        zero_kernel, (WIDE, NARROW, table, jax.ShapeDtypeStruct((RING, 512, 256), BF16)), (), region[0]
    )
    halo, (zero, zero_narrow, bd1, bd2) = halo_of(*region, early)
    ops_shape = jax.ShapeDtypeStruct((2, 7, RING * T, T), F32)
    ops = local(operators_kernel, ops_shape, (flags,), *packs)
    bd1, ops = local(near_kernel, (table, ops_shape), (flags,), *halo[:4], bd1, ops, alias={5: 0, 6: 1})
    idx, bd1, ops = local(
        cross_kernel,
        (jax.ShapeDtypeStruct((IDX_ROWS, T), jnp.int32), table, ops_shape),
        (flags,),
        *halo,
        bd1,
        ops,
        scratch=[pltpu.VMEM((2, 24, T), jnp.int32)],
        alias={7: 1, 8: 2},
    )

    tables = (bd1, bd2, ops)
    one, *one_blocks = step(True, False, True, True, flags, idx, (zero_narrow, *halo[1:]), *tables)
    *two_blocks, part0, part1, part2, part3 = halved_step(
        False, flags, idx, halo_of(*one_blocks)[0], tables, zero
    )
    got = ring_exchanged((part0, part1, part2, part3))
    three_parts = halved_step(True, flags, idx, halo_of(*two_blocks)[0], tables, one)
    three_parts, got = lax.optimization_barrier((three_parts, got))
    two_a, two_b = results(flags, got, ((0,), (1, 2, 3)))
    three_a, three_b = results(flags, ring_exchanged(three_parts), ((0,), (1,), (2,), (3,)))
    return two_a, two_b, three_a, three_b


def solution(mesh):
    field = P(None, None, "gx", "gy")
    site = P(None, "gx", "gy")
    out = P(None, None, None, "gx", "gy")
    return jax.shard_map(
        body,
        mesh=mesh,
        in_specs=(
            field,
            field,
            site,
            site,
            site,
            site,
            P("gx", "gy", None, None, None, None, None),
            P("gx", "gy", None),
            P("gx", "gy", None),
            P("gx", "gy"),
        ),
        out_specs=(out, out, out, out),
        check_vma=False,
    )
```

```python
import functools
import math

import jax
import jax.numpy as jnp
from jax import lax
from jax.experimental import pallas as pl
from jax.experimental.pallas import tpu as pltpu
from jax.sharding import PartitionSpec as P

RING = 4
T = 128
KS = 8
SR = 16
HALO = RING + 2
HOMES = HALO * 3
F32 = jnp.float32
BF16 = jnp.bfloat16
I16 = jnp.int16
PHASE_UNIT = math.pi / 32768.0
HOP_MID, HOP_UNIT = 0.12, 0.04 / 32767.0
SITE_UNIT = 0.25 / 32767.0
COUPLING_UNIT = 0.3 / 32767.0
VMEM_LIMIT = 28 * 1024 * 1024


PHASE_ROWS = 4 * T
ROW_EDGE, COL_EDGE, CODE, AT = 64, 66, 68, 69
SMALL_ROWS = 80
CARGO = PHASE_ROWS + SMALL_ROWS
LAND, ANY, SRC_ROW, SRC_COL, USED = 0, 24, 48, 72, 96
IDX_ROWS = 120


def coded(values, unit):
    return jnp.clip(jnp.round(values * (1.0 / unit)), -32768.0, 32767.0).astype(jnp.int32).astype(I16)


def decoded(code):
    return code.astype(jnp.int32).astype(F32)


def moved(array, axis, by):
    size = lax.axis_size(axis)
    return lax.ppermute(array, axis, [(i, i + by) for i in range(size) if 0 <= i + by < size])


def ring_moved(array, by):
    size = lax.axis_size("gx")
    pairs = [(i, i // RING * RING + (i + by) % RING) for i in range(size)]
    return lax.ppermute(array, "gx", pairs)


def lane_iota(shape, dim):
    return lax.broadcasted_iota(jnp.int32, shape, dim)


def started(copies, sems):
    copies = [pltpu.make_async_copy(source, to, sems.at[n]) for n, (source, to) in enumerate(copies)]
    for copy in copies:
        copy.start()
    return copies


def encode_kernel(flags, coupling, phase_one, phase_two, hop_one, hop_two, *refs):
    outs, (held, first_row, bonds, sems) = refs[:RING], refs[RING:]
    hops, phases = (hop_one, hop_two), (phase_one, phase_two)
    pending = started(
        [(hops[n].at[1, 0:8, :], first_row.at[n]) for n in range(2)]
        + [(hops[n].at[2], bonds.at[n]) for n in range(2)]
        + [(phases[n].at[(flags[0, 0] + d) % RING], held.at[d, n]) for d in range(RING) for n in range(2)],
        sems,
    )
    for copy in pending[:4]:
        copy.wait()
    live = flags[0, 8]
    lane = lane_iota((1, T), 1)
    code = jnp.zeros((1, T), jnp.int32)
    at = jnp.zeros((1, T), jnp.int32)
    for k in range(KS):
        owner, target = flags[0, 10 + k], flags[0, 10 + KS + k]
        strip = (owner // flags[0, 9] - flags[0, 5] + 1) * 4 + owner % flags[0, 9] - flags[0, 6] + 1
        here = (lane == k) & (k < live)
        code = jnp.where(here, strip + 16, code)
        at = jnp.where(here, target, at)
    weights = jnp.where(lane_iota((32, 256), 1) // 32 < live, coupling[...].T, 0.0)
    weights = coded(weights, COUPLING_UNIT)
    edges = [first_row[n, 0:1, :] for n in range(2)] + [bonds[n].T[0:1, :] for n in range(2)]
    edges = coded(jnp.concatenate(edges + [jnp.zeros((12, T), F32)], 0) - HOP_MID, HOP_UNIT).astype(jnp.int32)
    row = lane_iota((16, T), 0)
    words = jnp.where(row == CODE - 64, code, jnp.where(row == AT - 64, at, jnp.where(row < 4, edges, 0)))
    for d, out in enumerate(outs):
        for layer in range(2):
            pending[4 + d * 2 + layer].wait()
            for a in range(2):
                to = (layer * 2 + a) * T
                out[to : to + T, :] = coded(held[d, layer, a], PHASE_UNIT)
        out[PHASE_ROWS : PHASE_ROWS + 32, :] = weights[:, :T]
        out[PHASE_ROWS + 32 : PHASE_ROWS + 64, :] = weights[:, T:]
        out[PHASE_ROWS + 64 :, :] = words.astype(I16)


def pack_kernel(hop_one, hop_two, onsite_one, onsite_two, out, held, sems):
    fields = ((hop_one, onsite_one), (hop_two, onsite_two))
    pending = started(
        [
            (hop.at[n] if n < 3 else site.at[n - 3], held.at[layer, n])
            for layer, (hop, site) in enumerate(fields)
            for n in range(5)
        ],
        sems,
    )
    for layer in range(2):
        for n in range(5):
            at = layer * 5 + n
            pending[at].wait()
            value = held[layer, n]
            value = coded(value - HOP_MID, HOP_UNIT) if n < 3 else coded(value, SITE_UNIT)
            out[at * T : (at + 1) * T, :] = value


def region_kernel(flags, part0, part1, part2, part3, region, *edge_blocks):
    z = flags[0, 0]
    for d, part in enumerate((part0, part1, part2, part3)):
        region[(z + RING - d) % RING] = part[...]
    for slot in range(2):
        edge_blocks[slot][...] = region[edge_row(flags, slot) // (HALO - 1) * (RING - 1)]


def operators_kernel(flags, own, other, far, ops):
    z = flags[0, 0]
    blocks = ((own, z), (other, z + 1 - z % 2 * 2), (far.at[0], 3 - z), (far.at[1], 2 + z % 2 * 2 - z))
    for part, place in blocks:
        at = pl.ds(pl.multiple_of(place * T, T), T)
        for layer in range(2):
            for n in range(5):
                base = (layer * 5 + n) * T
                raw = decoded(part[base : base + T, :])
                ops[layer, n, at, :] = raw * HOP_UNIT + HOP_MID if n < 3 else raw * SITE_UNIT


OWN, CROSS, NEAR = 0, 1, 2


def neighbourhood(own, ends, near, near_ends, cross, cross_ends):
    def block(row, side):
        if row in SLOTS:
            return (ends, cross_ends, near_ends)[side].at[SLOTS.index(row)]
        return (own, cross, near)[side].at[row - 1]

    return block


SLOTS = ("A", "B")
ROWS = (1, 2, 3, 4) + SLOTS


def edge_row(flags, slot):
    return flags[0, 7] if slot == 0 else HALO - 1 - flags[0, 7]


def row_of(flags, row):
    return edge_row(flags, SLOTS.index(row)) if row in SLOTS else row


def rows_of(rb):
    if isinstance(rb, int):
        return slice(rb * T, (rb + 1) * T)
    return pl.ds(pl.multiple_of(rb * T, T), T)


def column_of(flags, side):
    return 1 if side == OWN else flags[0, 3] if side == CROSS else 2 - flags[0, 3]


def coupling_tables(ref, home, bd1, bd2=None, n=None):
    rows, cols = lane_iota((32, 256), 0), lane_iota((32, 256), 1)
    place = ((rows // 16 == cols // 128) & (rows % 16 == cols % 16)).astype(BF16)
    i, j = lane_iota((256, 256), 0), lane_iota((256, 256), 1)
    mask1 = (i // 32) == ((j // 16) % 8)
    mask2 = ((i // 16) % 8) == (j // 32)
    first = (((0,), (0,)), ((), ()))

    def spread(a, b, mask):
        full = lax.dot_general(a, b, first, preferred_element_type=F32)
        return jnp.where(mask, full, 0.0).astype(BF16)

    c = jnp.concatenate([decoded(ref[PHASE_ROWS + m : PHASE_ROWS + m + 32, :]) for m in (0, 32)], 1)
    c = c * COUPLING_UNIT
    high = c.astype(BF16)
    low = (c - high.astype(F32)).astype(BF16)
    bd1[home, 0:256, :] = spread(high, place, mask1)
    bd1[home, 256:512, :] = spread(low, place, mask1)
    if bd2 is not None:
        bd2[n, 0:256, :] = spread(place, high, mask2)
        bd2[n, 256:512, :] = spread(place, low, mask2)


def near_kernel(flags, own, ends, near, near_ends, bd1_in, ops_in, bd1, ops):
    block = neighbourhood(own, ends, near, near_ends, None, None)
    for side in (OWN, NEAR):
        for row in SLOTS if side == OWN else ROWS:
            coupling_tables(block(row, side), row_of(flags, row) * 3 + column_of(flags, side), bd1)
    lane = lane_iota((T, T), 1)
    for layer in range(2):
        ops[layer, 5, 0 : RING * T - 1, :] = ops[layer, 1, 1 : RING * T, :]
        below = [bond_edge(block(slot, OWN), ROW_EDGE + layer) for slot in SLOTS]
        ops[layer, 5, RING * T - 1 : RING * T, :] = jnp.where(
            jnp.broadcast_to(flags[0, 7], (1, T)) == HALO - 1, below[0], below[1]
        )
        for r in range(RING):
            column = jnp.broadcast_to(bond_edge(near.at[r], COL_EDGE + layer), (T, T)).T
            ops[layer, 6, rows_of(r), :] = jnp.where(
                lane == T - 1, column, pltpu.roll(ops[layer, 2, rows_of(r), :], T - 1, 1)
            )


def bond_edge(ref, row):
    words = decoded(ref[PHASE_ROWS + 64 : PHASE_ROWS + 80, :])
    return words[row - 64 : row - 63, :] * HOP_UNIT + HOP_MID


def cross_kernel(flags, *refs):
    idx, bd1, ops, codes = refs[8:]
    block = neighbourhood(*refs[:6])
    for row in ROWS:
        coupling_tables(block(row, CROSS), row_of(flags, row) * 3 + column_of(flags, CROSS), bd1)
    lane = lane_iota((T, T), 1)
    is_right = flags[0, 3] == 2
    for layer in range(2):
        for r in range(RING):
            column = jnp.broadcast_to(bond_edge(block(r + 1, CROSS), COL_EDGE + layer), (T, T)).T
            ops[layer, 6, rows_of(r), :] = jnp.where(
                (lane == T - 1) & is_right, column, ops[layer, 6, rows_of(r), :]
            )

    codes[...] = jnp.zeros_like(codes)
    for side in (OWN, CROSS, NEAR):
        for row in ROWS:
            home = row_of(flags, row) * 3 + column_of(flags, side)
            words = block(row, side)[PHASE_ROWS + 64 : PHASE_ROWS + 80, :].astype(jnp.int32)
            codes[0, pl.ds(home, 1), :] = words[CODE - 64 : CODE - 63, :]
            codes[1, pl.ds(home, 1), :] = words[AT - 64 : AT - 63, :]

    code, at = codes[0], codes[1]
    home = lane_iota((24, T), 0)
    active = code >= 16
    rb = home // 3 + jnp.where(active, ((code >> 2) & 3) - 1, 0)
    cb = home % 3 + jnp.where(active, (code & 3) - 1, 0)
    lands = active & (cb == 1) & (rb >= 1) & (rb <= RING)
    idx[LAND : LAND + 24, :] = jnp.where(lands, (rb - 1) * T + at, -1)
    some = jnp.max(jnp.where(lands, 1.0, 0.0), axis=1, keepdims=True)
    idx[ANY : ANY + 24, :] = jnp.broadcast_to(some, (24, T)).astype(jnp.int32)
    idx[SRC_ROW : SRC_ROW + 24, :] = jnp.clip(rb * T + at, 0, HALO * T - SR)
    idx[SRC_COL : SRC_COL + 24, :] = jnp.clip(cb, 0, 2)
    mine = active & (home % 3 == 1) & (home // 3 >= 1) & (home // 3 <= RING)
    source = jnp.where(mine, rb * 3 + cb, -1)
    idx[USED : USED + 24, :] = jnp.zeros((24, T), jnp.int32)
    for n in range(HOMES):
        hit = jnp.where(source == n, 1.0, 0.0)
        used = jnp.max(jnp.max(hit, axis=1, keepdims=True), axis=0, keepdims=True)
        idx[USED + n : USED + n + 1, :] = jnp.broadcast_to(used, (1, T)).astype(jnp.int32)


def cos_sin(code):
    q = code.astype(jnp.int32)
    quarter = (q + 8192) >> 14
    r = (q - (quarter << 14)).astype(F32) * PHASE_UNIT
    r2 = r * r
    s = r * (1.0 + r2 * (-1.6666654611e-1 + r2 * (8.3321608736e-3 + r2 * -1.9515295891e-4)))
    c = 1.0 + r2 * (-0.5 + r2 * (4.166664568298827e-2 + r2 * (-1.388731625493765e-3 + r2 * 2.443315711809948e-5)))
    odd = (quarter & 1) == 1
    cos_v = jnp.where(odd, s, c)
    sin_v = jnp.where(odd, c, s)
    cos_v = jnp.where(((quarter + 1) & 2) == 2, -cos_v, cos_v)
    sin_v = jnp.where((quarter & 2) == 2, -sin_v, sin_v)
    return cos_v, sin_v


def zero_kernel(region, zero_out, narrow_out, bd1, bd2):
    for rb in range(RING):
        coupling_tables(region.at[rb], (rb + 1) * 3 + 1, bd1, bd2, rb)
        for layer in range(2):
            for a in range(2):
                at = (layer * 2 + a) * T
                pair = cos_sin(region[rb, at : at + T, :])
                for p in range(2):
                    zero_out[layer, a, p, rows_of(rb), :] = pair[p]
                    narrow_out[rb, layer, a * T : (a + 1) * T, p * T : (p + 1) * T] = pair[p].astype(BF16)


def step_kernel(first, last, begin, end, *refs):
    refs = list(refs)
    flags, idx = refs[:2]
    refs = refs[2:]
    own = ends = cross = cross_ends = near = near_ends = sums_in = sums_out = prev = wide_out = narrow_out = None
    if begin:
        own, ends, near, near_ends = refs[:4]
        refs = refs[4:]
    if end:
        cross, cross_ends = refs[:2]
        refs = refs[2:]
    around = neighbourhood(own, ends, near, near_ends, cross, cross_ends)
    bd1, bd2, ops = refs[:3]
    refs = refs[3:]
    sides = (OWN, NEAR) * begin + (CROSS,) * end
    far_column = column_of(flags, CROSS)
    here = [(begin and end) or (column_of(flags, CROSS if end else NEAR) == cb) for cb in (0, 2)]
    if end and not begin:
        sums_in = refs.pop(0)
    if end and not first:
        prev = refs.pop(0)
    if first:
        wide_out = refs.pop(0)
    edge_blocks, parts = [], []
    if not end:
        sums_out = refs.pop(0)
    elif last:
        parts = refs[:RING]
        refs = refs[RING:]
        narrow_out = refs.pop()
    else:
        narrow_out, *edge_blocks = refs[:3]
        refs = refs[3:]
    fu, fv, fvs, gathered, sources, terms_a, terms_b, acc1, acc2, homes, count = refs[:11]
    xv = refs[11] if first else None

    def halves(p):
        return slice(p * T, (p + 1) * T)

    def decode(layer, row, side, a, edge):
        at = pl.multiple_of((layer * 2 + a) * T, T)
        pair = cos_sin(around(row, side)[pl.ds(at, T), :])
        if side == OWN:
            factor = flags[0, 1 + SLOTS.index(row)].astype(F32)
        else:
            factor = flags[0, 4].astype(F32) if side == CROSS else 1.0
        rb, cb = row_of(flags, row), column_of(flags, side)
        for p in range(2):
            value = (pair[p] * factor).astype(BF16)
            if layer == 0:
                fu[cb, a, p, rows_of(rb), :] = value.astype(F32)
                continue
            xv[rb * 3 + cb, pl.ds(pl.multiple_of(a * T, T), T), halves(p)] = value
            if side == OWN:
                fv[a, p, rows_of(rb), :] = value.astype(F32)
            elif edge:
                fvs[cb // 2, p, rows_of(rb - 1), :] = value.astype(F32)

    def widen(layer, row, side, a, edge):
        ref = around(row, side).at[layer]
        at = pl.ds(pl.multiple_of(a * T, T), T)
        rb, cb = row_of(flags, row), column_of(flags, side)
        for p in range(2):
            value = ref[at, halves(p)].astype(F32)
            if layer == 0:
                fu[cb, a, p, rows_of(rb), :] = value
            elif side == OWN:
                fv[a, p, rows_of(rb), :] = value
            elif edge:
                fvs[cb // 2, p, rows_of(rb - 1), :] = value

    for side, row in [(side, row) for side in sides for row in ROWS]:
        cb = column_of(flags, side)
        for layer in range(2):
            if side == OWN and row not in SLOTS:
                for a in range(2):
                    widen(layer, row, side, a, False)
                continue
            edge = None
            if side == OWN:
                edge = 1 - row_of(flags, row) // (HALO - 1)
            elif row not in SLOTS:
                edge = 1 - cb // 2
            load = decode if first else widen
            if edge is not None:
                load(layer, row, side, edge, True)
            if layer == 1 and not first:
                continue

            @pl.when(idx[(USED if layer == 0 else ANY) + row_of(flags, row) * 3 + cb, 0] > 0)
            def _():
                for a in range(2) if edge is None else (1 - edge,):
                    load(layer, row, side, a, False)

    if sums_in is not None:
        acc1[:, :, 0 : RING * T, :] = sums_in[0]
        acc2[...] = sums_in[1]
    else:
        acc1[...] = jnp.zeros_like(acc1)
        acc2[...] = jnp.zeros_like(acc2)
    for r in range(RING):
        home = (r + 1) * 3 + 1
        columns = [idx[SRC_COL + home, k] for k in range(KS)]
        wanted = [(col == far_column) if end else (col != far_column) for col in columns]
        for k in range(KS):
            source = idx[SRC_ROW + home, k]
            for a in range(2):
                for p in range(2):
                    piece = fu[columns[k], a, p, pl.ds(source, SR), :]
                    if not (begin and end):
                        piece = jnp.where(wanted[k], piece, 0.0)
                    gathered[r, k * 32 + a * SR : k * 32 + (a + 1) * SR, halves(p)] = piece.astype(BF16)
    for r in range(RING):
        both = jnp.dot(bd2[r], gathered[r], preferred_element_type=F32)
        summed = both[:256] + both[256:]
        for b in range(2):
            for p in range(2):
                acc2[b, p, rows_of(r), :] += summed[b * T : (b + 1) * T, halves(p)]

    count[0] = 1
    homes[0] = HOMES
    for side, row in [(side, row) for side in sides for row in ROWS]:
        home = row_of(flags, row) * 3 + column_of(flags, side)

        @pl.when(idx[ANY + home, 0] > 0)
        def _():
            n = count[0]
            decoded_here = first and (side != OWN or row in SLOTS)
            sources[n] = xv[home] if decoded_here else around(row, side)[1]
            homes[n] = home
            count[0] = n + 1

    homes[count[0]] = HOMES

    def product(n):
        both = jnp.dot(bd1[jnp.minimum(homes[n], HOMES - 1)], sources[n], preferred_element_type=F32)
        return both[:256] + both[256:]

    def scatter(n, held):
        for k in range(KS):
            landing = idx[LAND + homes[n], k]
            landing = jnp.where(landing < 0, RING * T, landing)
            for a in range(2):
                for p in range(2):
                    at = (a, p, pl.ds(landing, SR), slice(None))
                    acc1[at] = acc1[at] + held[k * 32 + a * SR : k * 32 + (a + 1) * SR, halves(p)]

    def pair(j, carry):
        terms_a[...] = product(2 * j + 1)
        scatter(2 * j, terms_b)
        terms_b[...] = product(2 * j + 2)
        scatter(2 * j + 1, terms_a)
        return carry

    pairs = count[0] // 2
    lax.fori_loop(0, pairs, pair, 0)
    scatter(2 * pairs, terms_b)

    lane = lane_iota((T, T), 1)
    for layer in range(2):
        acc = (acc1, acc2)[layer]

        def field(a, p, low):
            if layer == 0:
                return fu[1, a, p, low : low + T, :]
            return fv[a, p, low : low + T, :]

        def beside(a, p, r, cb):
            if layer == 0:
                return fu[cb, a, p, (r + 1) * T : (r + 2) * T, :]
            return fvs[cb // 2, p, r * T : (r + 1) * T, :]

        for r in range(RING):
            rows = rows_of(r)
            h0, h1, h2, e0, e1, h1s, h2s = [ops[layer, n, rows, :] for n in range(7)]
            for p in range(2):
                upper, lower = acc[0, p, rows, :], acc[1, p, rows, :]
                before = jnp.where((lane == 0) & here[0], pltpu.roll(beside(1, p, r, 0), 1, 1), 0.0)
                after = jnp.where((lane == T - 1) & here[1], pltpu.roll(beside(0, p, r, 2), T - 1, 1), 0.0)
                if begin:
                    base = (r + 1) * T
                    w0, w1 = field(0, p, base), field(1, p, base)
                    upper = upper + (e0 * w0 + h0 * w1 + h1 * field(1, p, base - 1))
                    lower = lower + (e1 * w1 + h0 * w0 + h1s * field(0, p, base + 1))
                    before = jnp.where(lane == 0, before, pltpu.roll(w1, 1, 1))
                    after = jnp.where(lane == T - 1, after, pltpu.roll(w0, T - 1, 1))
                upper = upper + h2 * before
                lower = lower + h2s * after
                for a, value in enumerate((upper, lower)):
                    if not end:
                        sums_out[layer, a, p, rows, :] = value
                        continue
                    if first:
                        wide_out[layer, a, p, rows, :] = value
                    else:
                        value = 2.0 * value - prev[layer, a, p, rows, :]
                    narrow_out[r, layer, a * T : (a + 1) * T, halves(p)] = value.astype(BF16)

    if edge_blocks:
        for slot in range(2):
            edge_blocks[slot][...] = narrow_out[edge_row(flags, slot) // (HALO - 1) * (RING - 1)]
    for d, part in enumerate(parts):
        part[...] = narrow_out[(flags[0, 0] + d) % RING]


def parts_kernel(flags, narrow, *parts):
    for d, part in enumerate(parts):
        part[...] = narrow[(flags[0, 0] + d) % RING]


def result_kernel(shifts, flags, *refs):
    parts, refs = refs[: len(shifts)], refs[len(shifts) :]
    if shifts[0]:
        refs = refs[2:]
    outs, (held, sems) = refs[:2], refs[2:]
    pending = []
    for n, (d, part) in enumerate(zip(shifts, parts)):
        state = (flags[0, 0] + RING - d) % RING
        for layer, out in enumerate(outs):
            for p in range(2):
                for a in range(2):
                    value = part[layer, a * T : (a + 1) * T, p * T : (p + 1) * T]
                    held[n, layer, p, a] = value.astype(F32)
            copy = pltpu.make_async_copy(held.at[n, layer], out.at[state], sems.at[n * 2 + layer])
            copy.start()
            pending.append(copy)
    for copy in pending:
        copy.wait()


HBM = pl.BlockSpec(memory_space=pltpu.HBM)
SMEM = pl.BlockSpec(memory_space=pltpu.SMEM)
VMEM = pl.BlockSpec(memory_space=pltpu.VMEM)
PARAMS = pltpu.CompilerParams(vmem_limit_bytes=VMEM_LIMIT)
WIDE = jax.ShapeDtypeStruct((2, 2, 2, RING * T, T), F32)
NARROW = jax.ShapeDtypeStruct((RING, 2, 2 * T, 2 * T), BF16)
BLOCK = jax.ShapeDtypeStruct((2, 2 * T, 2 * T), BF16)


def local(kernel, out_shape, scalars, *operands, far=(), scratch=(), cost=None, alias=None):
    return pl.pallas_call(
        kernel,
        out_shape=out_shape,
        in_specs=[SMEM] * len(scalars) + [VMEM] * len(operands) + [HBM] * len(far),
        out_specs=jax.tree.map(lambda _: VMEM, out_shape),
        scratch_shapes=list(scratch),
        compiler_params=PARAMS,
        cost_estimate=cost,
        input_output_aliases=alias or {},
    )(*scalars, *operands, *(pltpu.with_memory_space_constraint(x, pltpu.HBM) for x in far))


def step(first, last, begin, end, flags, idx, halo, *rest):
    scratch = [
        pltpu.VMEM((3, 2, 2, HALO * T, T), F32),
        pltpu.VMEM((2, 2, HALO * T, T), F32),
        pltpu.VMEM((2, 2, RING * T, T), F32),
        pltpu.VMEM((RING, 2 * T, 2 * T), BF16),
        pltpu.VMEM((HOMES + 2, 2 * T, 2 * T), BF16),
        pltpu.VMEM((2 * T, 2 * T), F32),
        pltpu.VMEM((2 * T, 2 * T), F32),
        pltpu.VMEM((2, 2, RING * T + SR, T), F32),
        pltpu.VMEM((2, 2, RING * T, T), F32),
        pltpu.SMEM((HOMES + 2,), jnp.int32),
        pltpu.SMEM((1,), jnp.int32),
    ]
    if first:
        scratch.append(pltpu.VMEM((HOMES, 2 * T, 2 * T), BF16))
        out = (WIDE, NARROW, BLOCK, BLOCK)
    elif not end:
        out = WIDE
    elif last:
        scratch.append(pltpu.VMEM(NARROW.shape, BF16))
        out = (BLOCK,) * RING
    else:
        out = (NARROW, BLOCK, BLOCK)
    halo = halo[: 6 if end else 4][0 if begin else 4 :]
    kernel = functools.partial(step_kernel, first, last, begin, end)
    moved_bytes = sum(math.prod(x.shape) * x.dtype.itemsize for x in (*halo, *rest, *jax.tree.leaves(out)))
    products = 2 * (RING + HALO) * 512 * 256 * 256
    cost = pl.CostEstimate(flops=products, bytes_accessed=moved_bytes, transcendentals=0)
    return local(kernel, out, (flags, idx), *halo, *rest, scratch=scratch, cost=cost)


def halved_step(last, flags, idx, halo, tables, prev):
    sums = step(False, last, True, False, flags, idx, halo, *tables)
    return step(False, last, False, True, flags, idx, halo, *tables, sums, prev)


def across(array, low):
    size = lax.axis_size("gy")
    pairs = [(i, i + 1) for i in range(low, size - 1, 2)]
    return lax.ppermute(array, "gy", pairs + [(j, i) for i, j in pairs])


def swapped_rows(array, low):
    size = lax.axis_size("gx")
    pairs = [(i, i + RING) for i in range(size - RING) if i // RING % 2 == low]
    return lax.ppermute(array, "gx", pairs + [(j, i) for i, j in pairs])


def halo_of(region, block_a, block_b, beside=()):
    cross, near = across(region, 1), across(region, 0)
    ends = jnp.stack([swapped_rows(block_a, 0), swapped_rows(block_b, 1)])
    ends, beside = lax.optimization_barrier((ends, beside))
    return (region, ends, near, across(ends, 0), cross, across(ends, 1)), beside


def ring_swapped(array, partner):
    size = lax.axis_size("gx")
    pairs = [(i, i // RING * RING + partner[i % RING]) for i in range(size)]
    return lax.ppermute(array, "gx", pairs)


def ring_exchanged(parts):
    return [parts[0]] + [ring_moved(parts[d], d) for d in range(1, RING)]


def written(flags, shifts, parts, before=()):
    count = len(shifts)
    return pl.pallas_call(
        lambda *refs: result_kernel(shifts, *refs),
        out_shape=(jax.ShapeDtypeStruct((RING, 2, 2, T, T), F32),) * 2,
        in_specs=[SMEM] + [VMEM] * count + [HBM] * len(before),
        out_specs=(HBM, HBM),
        scratch_shapes=[pltpu.VMEM((count, 2, 2, 2, T, T), F32), pltpu.SemaphoreType.DMA((2 * count,))],
        input_output_aliases={1 + count + n: n for n in range(len(before))},
        compiler_params=PARAMS,
    )(flags, *parts, *before)


def results(flags, parts, groups):
    out = ()
    for shifts in groups:
        out = written(flags, shifts, [parts[d] for d in shifts], out)
    return out


def body(phase_one, phase_two, hop_one, hop_two, onsite_one, onsite_two, coupling, owner, target_row, live_strips):
    grid_row, grid_col = lax.axis_index("gx"), lax.axis_index("gy")
    rows_n, cols_n = lax.axis_size("gx"), lax.axis_size("gy")
    odd, ring = grid_col % 2, grid_row // RING
    crossing = jnp.where(odd == 1, grid_col < cols_n - 1, grid_col > 0)
    second = jnp.where(ring % 2 == 1, ring < rows_n // RING - 1, ring > 0)
    first_row = jnp.where(ring % 2 == 1, 0, HALO - 1)
    flags = [grid_row % RING, ring // 2 * 2 + 1 < rows_n // RING, second, 2 * odd, crossing, grid_row, grid_col]
    flags += [first_row, live_strips[0, 0], cols_n]
    flags = [jnp.asarray(f).astype(jnp.int32).reshape(1) for f in flags]
    flags = jnp.concatenate(flags + [owner[0, 0], target_row[0, 0]]).reshape(1, 10 + 2 * KS)

    cargo = jax.ShapeDtypeStruct((CARGO, T), I16)
    sends = local(
        encode_kernel,
        (cargo,) * RING,
        (flags,),
        coupling.reshape(2 * KS * SR, 2 * SR),
        far=(phase_one, phase_two, hop_one, hop_two),
        scratch=[
            pltpu.VMEM((RING, 2, 2, T, T), F32),
            pltpu.VMEM((2, 8, T), F32),
            pltpu.VMEM((2, T, T), F32),
            pltpu.SemaphoreType.DMA((4 + 2 * RING,)),
        ],
    )
    parts = ring_exchanged(sends)
    packed = local(
        pack_kernel,
        jax.ShapeDtypeStruct((10 * T, T), I16),
        (),
        far=(hop_one, hop_two, onsite_one, onsite_two),
        scratch=[pltpu.VMEM((2, 5, T, T), F32), pltpu.SemaphoreType.DMA((10,))],
    )
    other = ring_swapped(packed, (1, 0, 3, 2))
    parts, other = lax.optimization_barrier((parts, other))

    region = local(
        region_kernel, (jax.ShapeDtypeStruct((RING, CARGO, T), I16), cargo, cargo), (flags,), *parts
    )
    region, both = lax.optimization_barrier((region, jnp.stack([packed, other])))
    packs = (packed, other, ring_swapped(both, (3, 2, 1, 0)))
    table = jax.ShapeDtypeStruct((HOMES, 512, 256), BF16)
    early = local(
        zero_kernel, (WIDE, NARROW, table, jax.ShapeDtypeStruct((RING, 512, 256), BF16)), (), region[0]
    )
    halo, (zero, zero_narrow, bd1, bd2) = halo_of(*region, early)
    ops_shape = jax.ShapeDtypeStruct((2, 7, RING * T, T), F32)
    ops = local(operators_kernel, ops_shape, (flags,), *packs)
    bd1, ops = local(near_kernel, (table, ops_shape), (flags,), *halo[:4], bd1, ops, alias={5: 0, 6: 1})
    idx, bd1, ops = local(
        cross_kernel,
        (jax.ShapeDtypeStruct((IDX_ROWS, T), jnp.int32), table, ops_shape),
        (flags,),
        *halo,
        bd1,
        ops,
        scratch=[pltpu.VMEM((2, 24, T), jnp.int32)],
        alias={7: 1, 8: 2},
    )

    tables = (bd1, bd2, ops)
    one, *one_blocks = step(True, False, True, True, flags, idx, (zero_narrow, *halo[1:]), *tables)
    two_blocks = halved_step(
        False, flags, idx, halo_of(*one_blocks)[0], tables, zero
    )
    got = ring_exchanged(local(parts_kernel, (BLOCK,) * RING, (flags,), two_blocks[0]))
    three_parts = halved_step(True, flags, idx, halo_of(*two_blocks)[0], tables, one)
    three_parts, got = lax.optimization_barrier((three_parts, got))
    two_a, two_b = results(flags, got, ((0,), (1, 2, 3)))
    three_a, three_b = results(flags, ring_exchanged(three_parts), ((0,), (1,), (2,), (3,)))
    return two_a, two_b, three_a, three_b


def solution(mesh):
    field = P(None, None, "gx", "gy")
    site = P(None, "gx", "gy")
    out = P(None, None, None, "gx", "gy")
    return jax.shard_map(
        body,
        mesh=mesh,
        in_specs=(
            field,
            field,
            site,
            site,
            site,
            site,
            P("gx", "gy", None, None, None, None, None),
            P("gx", "gy", None),
            P("gx", "gy", None),
            P("gx", "gy"),
        ),
        out_specs=(out, out, out, out),
        check_vma=False,
    )
```
